256 devices in a mesh: img: 16 (over x, y), proto: 16 (over z, core).
Axes of the slice: x: 4, y: 4, z: 8, core: 2. Of those that a mesh axis runs over, the one named last changes fastest.
Arguments:
- student_patch_tokens: bfloat16 [16, 256, 4096], P('img', None, 'proto'), may hold values from -6 to 6
- teacher_patch_tokens: bfloat16 [16, 256, 4096], P('img', None, 'proto'), may hold values from -6 to 6
- mask_counts: int32 [16], P('img'), may hold values from 32 to 128, as said below
- mask_index: int32 [16, 128], P('img'), may hold values from 0 to 255, as said below
- student_bottleneck: bfloat16 [4096, 256], P('proto'), may hold values from -0.09375 to 0.09375
- teacher_bottleneck: bfloat16 [4096, 256], P('proto'), may hold values from -0.09375 to 0.09375
- student_protos: bfloat16 [256, 98304], P(None, 'proto'), may hold values from -60 to 60
- teacher_protos: bfloat16 [256, 98304], P(None, 'proto'), may hold values from -60 to 60
- center: float32 [98304], P('proto'), may hold values from -0.75 to 0.75
Outputs:
- image_loss: float32 [16], P('img')
- grad_protos: float32 [256, 98304], P('img', 'proto')
- grad_bottleneck: float32 [4096, 256], P('proto', 'img')
The draws below stay inside these ranges and needn't reach their ends.
Inputs may be any that keep to these rules, and one draw needn't show every extreme that they name: `mask_counts`: some image has exactly 128 masked patches. `mask_index`: the 128 entries of an image are distinct patch numbers; only the first mask_counts of them are used.
All inputs are finite; a program needn't handle non-finite values.
Results may differ from the reference program's by a relative error of at most 0.0071.
Values may be sent and summed in bfloat16 or wider, within the bound.
A program may use at most 64 MiB of HBM per device.

```python
import math
import jax
import jax.numpy as jnp
from jax import lax

D = 4096
BOT = 256
PROTOS = 98304
PATCHES = 256
MASK_MAX = 128
IMAGES = 16


def draw_mask_counts(key, part):
    counts = jax.random.randint(key, (IMAGES,), MASK_MAX // 4, MASK_MAX + 1)
    chosen = jax.random.randint(jax.random.fold_in(key, 1), (), 0, IMAGES)
    counts = jnp.where(jnp.arange(IMAGES) == chosen, MASK_MAX, counts)
    return counts.astype(jnp.int32)


def draw_mask_index(key, part):
    keys = jax.random.split(jax.random.fold_in(key, 2), IMAGES)
    orders = jax.vmap(lambda single: jax.random.permutation(single, PATCHES))(keys)
    return orders[:, :MASK_MAX].astype(jnp.int32)


def proto_table(key):
    base = jax.random.normal(key, (BOT, PROTOS), jnp.float32) / math.sqrt(BOT)
    return jnp.clip(base, -60.0, 60.0)


def draw_student_protos(key, part):
    return proto_table(jax.random.fold_in(key, 11)).astype(jnp.bfloat16)


def draw_teacher_protos(key, part):
    return proto_table(jax.random.fold_in(key, 12)).astype(jnp.bfloat16)


def shard_levels(own_key, shape, pieces, least, high):
    def one(axis_at, parts):
        heights = jax.random.uniform(jax.random.fold_in(jax.random.fold_in(own_key, 6), axis_at), (parts,), jnp.float32, least / len(pieces), high / len(pieces))
        return jnp.repeat(jnp.exp(heights), shape[axis_at] // parts).reshape((-1,) + (1,) * (len(shape) - axis_at - 1))

    level = one(*pieces[0])
    for cut in pieces[1:]:
        level = level * one(*cut)
    return level


def gaussian(key, dims, width, limit, shards=(), kind=jnp.bfloat16):
    factor_of = shard_levels(key, dims, shards, -0.22, 0.18) if shards else 1.0
    entries = jax.random.normal(key, dims, jnp.float32) * width * factor_of
    return jnp.minimum(jnp.maximum(entries, -limit), limit).astype(kind)


def setup_inputs(seed: int = 0) -> dict:
    key_list = jax.random.split(jax.random.key(seed), 10)
    return {
        "student_patch_tokens": gaussian(key_list[0], (IMAGES, PATCHES, D), 1.0, 6.0, ((0, 16), (2, 16))),
        "teacher_patch_tokens": gaussian(key_list[1], (IMAGES, PATCHES, D), 1.0, 6.0, ((0, 16), (2, 16))),
        "mask_counts": draw_mask_counts(jax.random.fold_in(key_list[9], 71), 0),
        "mask_index": draw_mask_index(jax.random.fold_in(key_list[9], 71), 0),
        "student_bottleneck": gaussian(key_list[4], (D, BOT), D ** -0.5, 0.09375, ((0, 16),)),
        "teacher_bottleneck": gaussian(key_list[5], (D, BOT), D ** -0.5, 0.09375, ((0, 16),)),
        "student_protos": draw_student_protos(jax.random.fold_in(key_list[9], 71), 0),
        "teacher_protos": draw_teacher_protos(jax.random.fold_in(key_list[9], 71), 0),
        "center": gaussian(key_list[8], (PROTOS,), 0.05, 0.75, ((0, 16),), jnp.float32),
    }


EPSILON = 1e-06
STUDENT_TEMP = 0.1
TEACHER_TEMP = 0.04
LOSS_SCALE = 4096.0

def scores(units_student, units_teacher, weight, student_protos, teacher_protos, center):
    logits_student = jnp.dot(units_student, student_protos, preferred_element_type=jnp.float32) / STUDENT_TEMP
    logits_teacher = (jnp.dot(units_teacher, teacher_protos, preferred_element_type=jnp.float32) - center[None, :]) / TEACHER_TEMP
    top_student = lax.optimization_barrier(jnp.max(logits_student, axis=1))
    top_teacher = lax.optimization_barrier(jnp.max(logits_teacher, axis=1))
    exp_student = jnp.exp(logits_student - top_student[:, None])
    exp_teacher = jnp.exp(logits_teacher - top_teacher[:, None])
    total_student = lax.optimization_barrier(jnp.sum(exp_student, axis=1))
    total_teacher = lax.optimization_barrier(jnp.sum(exp_teacher, axis=1))
    cross = lax.optimization_barrier(jnp.sum(exp_teacher * logits_student, axis=1))
    loss_rows = -(cross / total_teacher - top_student - jnp.log(total_student))
    differ = exp_student / total_student[:, None] - exp_teacher / total_teacher[:, None]
    logit_gradient = (LOSS_SCALE * weight.astype(jnp.float32)[:, None] * differ / STUDENT_TEMP).astype(jnp.bfloat16)
    return (loss_rows, logit_gradient)

def reference(student_patch_tokens, teacher_patch_tokens, mask_counts, mask_index, student_bottleneck, teacher_bottleneck, student_protos, teacher_protos, center):
    picked = jnp.broadcast_to(mask_index[:, :, None], (IMAGES, MASK_MAX, D))
    student_token_rows = jnp.take_along_axis(student_patch_tokens, picked, axis=1).reshape(IMAGES * MASK_MAX, D)
    teacher_rows = jnp.take_along_axis(teacher_patch_tokens, picked, axis=1).reshape(IMAGES * MASK_MAX, D)
    hidden_student = jnp.dot(student_token_rows, student_bottleneck, preferred_element_type=jnp.float32)
    hidden_teacher = jnp.dot(teacher_rows, teacher_bottleneck, preferred_element_type=jnp.float32)
    inv_student = lax.rsqrt(lax.optimization_barrier(jnp.sum(hidden_student * hidden_student, axis=1, keepdims=True)) + EPSILON)
    inv_teacher = lax.rsqrt(lax.optimization_barrier(jnp.sum(hidden_teacher * hidden_teacher, axis=1, keepdims=True)) + EPSILON)
    units_student = (hidden_student * inv_student).astype(jnp.bfloat16)
    units_teacher = (hidden_teacher * inv_teacher).astype(jnp.bfloat16)
    position = lax.broadcasted_iota(jnp.int32, (IMAGES, MASK_MAX), 1)
    live = position < mask_counts[:, None]
    weight = jnp.where(live, 1.0 / mask_counts.astype(jnp.float32)[:, None], 0.0).astype(jnp.bfloat16)

    def block(proto_acc, items):
        unit_s, unit_t, weight_b = items
        loss_rows, logit_gradient = scores(unit_s, unit_t, weight_b, student_protos, teacher_protos, center)
        image_total = jnp.sum(weight_b.astype(jnp.float32) * loss_rows)
        proto_acc = proto_acc + jnp.dot(unit_s.T, logit_gradient, preferred_element_type=jnp.float32)
        grad_rows = jnp.dot(logit_gradient, student_protos.T, preferred_element_type=jnp.float32)
        return (proto_acc, (image_total, grad_rows))
    init = jnp.zeros((BOT, PROTOS), jnp.float32)
    items = (units_student.reshape(IMAGES, MASK_MAX, BOT), units_teacher.reshape(IMAGES, MASK_MAX, BOT), weight)
    grad_protos, (image_loss, grad_rows) = lax.scan(block, init, items)
    grad_rows = grad_rows.reshape(IMAGES * MASK_MAX, BOT)
    inner = lax.optimization_barrier(jnp.sum(hidden_student * grad_rows, axis=1, keepdims=True))
    grad_hidden = (grad_rows * inv_student - hidden_student * inner * (inv_student * inv_student * inv_student)).astype(jnp.bfloat16)
    grad_bottleneck = jnp.dot(student_token_rows.T, grad_hidden, preferred_element_type=jnp.float32)
    return (image_loss, grad_protos, grad_bottleneck)
```

```python
import functools

import jax
import jax.numpy as jnp
from jax import lax
from jax.experimental import pallas as pl
from jax.experimental.pallas import tpu as pltpu
from jax.sharding import PartitionSpec as P

EPSILON = 1e-06
STUDENT_SCALE = 10.0
TEACHER_SCALE = 25.0
GRAD_SCALE = 40960.0
MESH = pl.DeviceIdType.MESH
F32 = jnp.float32
BF16 = jnp.bfloat16

SIDE = 4
IMG = 16
ROWS = 128
BOT = 256
TILE = 512


def wait_bytes(ref, sem):
    pltpu.make_async_copy(ref, ref, sem).wait()


def kernel(
    tok_s_h,
    tok_t_h,
    cnt_ref,
    idx_h,
    bs_h,
    bt_h,
    ps_h,
    pt_h,
    cen_h,
    loss_ref,
    gp_ref,
    gb_ref,
    tok_s,
    tok_t,
    idx,
    bs,
    bt,
    ps,
    pt,
    cen,
    ps_own,
    pt_own,
    rows_s,
    a1_src,
    a1_recv,
    a2_src,
    a2_recv,
    hid,
    b_buf,
    units,
    ls_buf,
    lt_buf,
    st_buf,
    tot_buf,
    d_src,
    d_recv,
    e_buf,
    ps_own_t,
    pt_own_t,
    cen_own_t,
    g_acc,
    g_src,
    g_recv,
    f_src,
    f_recv,
    load_sem,
    a1_sem,
    a2_sem,
    b_sem,
    c_sem,
    t_sem,
    d_sem,
    e_sem,
    f_sem,
    g_sem,
    ag_send,
    ag_recv,
    sh_send,
    sh_recv,
):
    i = lax.axis_index("img")
    p = lax.axis_index("proto")
    x, y = i // SIDE, i % SIDE
    z, c = p // 2, p % 2
    width = ps_own.shape[1]
    tiles = ps.shape[1] // TILE

    barrier = pltpu.get_barrier_semaphore()

    def greet(k, carry):
        pl.semaphore_signal(barrier, inc=1, device_id=(i, (p + k) % 16), device_id_type=MESH)
        pl.semaphore_signal(barrier, inc=1, device_id=((i + k) % IMG, p), device_id_type=MESH)
        return carry

    lax.fori_loop(1, 16, greet, 0)

    own_columns = pl.ds(pl.multiple_of(i * width, 128), width)
    loads = [
        pltpu.make_async_copy(src, dst, load_sem.at[n])
        for n, (src, dst) in enumerate(
            (
                (idx_h, idx),
                (tok_s_h.at[0], tok_s),
                (bs_h, bs),
                (tok_t_h.at[0], tok_t),
                (bt_h, bt),
                (cen_h, cen),
                (ps_h.at[:, own_columns], ps_own),
                (pt_h.at[:, own_columns], pt_own),
                (ps_h, ps),
                (pt_h, pt),
            )
        )
    ]
    for load in loads:
        load.start()

    loads[0].wait()
    spread = jnp.broadcast_to(idx[...].astype(F32), (ROWS, ROWS)).T
    patch = lax.broadcasted_iota(jnp.int32, (ROWS, ROWS), 1).astype(F32)
    picker = jnp.concatenate(
        [(spread == patch).astype(F32), (spread == patch + 128.0).astype(F32)], axis=1
    ).astype(BF16)
    loads[1].wait()
    rows_s[...] = jnp.dot(picker, tok_s[...], preferred_element_type=F32).astype(BF16)
    loads[2].wait()
    part_s = jnp.dot(rows_s[...], bs[...], preferred_element_type=F32)
    loads[3].wait()
    rows_t = jnp.dot(picker, tok_t[...], preferred_element_type=F32).astype(BF16)
    loads[4].wait()
    part_t = jnp.dot(rows_t, bt[...], preferred_element_type=F32)
    a1_src[...] = jnp.where(c == 0, part_t, part_s)
    a2_src[...] = jnp.where(c == 0, part_s, part_t).reshape(8, 16, BOT)

    pl.semaphore_wait(barrier, 30)

    sibling = p + 1 - 2 * c
    a1 = pltpu.make_async_remote_copy(
        a1_src, a1_recv, a1_sem.at[0], a1_sem.at[1], device_id=(i, sibling), device_id_type=MESH
    )
    a1.start()
    loads[5].wait()
    loads[6].wait()
    ps_own_t[...] = ps_own[...].astype(F32).T.astype(BF16)
    loads[7].wait()
    pt_own_t[...] = pt_own[...].astype(F32).T.astype(BF16)
    for q in range(width // 128):
        cen_own_t[pl.ds(128 * q, 128), :] = jnp.broadcast_to(
            cen[pl.ds(i * (width // 128) + q, 1), :], (128, 128)
        ).T
    a1.wait_recv()
    a2_src[...] = a2_src[...] + a1_recv[...].reshape(8, 16, BOT)

    def a2_send(k, carry):
        z2 = (z + k) % 8
        pltpu.make_async_remote_copy(
            a2_src.at[z2],
            a2_recv.at[k - 1],
            a2_sem.at[0],
            a2_sem.at[1],
            device_id=(i, z2 * 2 + c),
            device_id_type=MESH,
        ).start()
        return carry

    lax.fori_loop(1, 8, a2_send, 0)
    wait_bytes(a2_recv, a2_sem.at[1])
    total = a2_src[z]
    for k in range(7):
        total = total + a2_recv[k]
    inv = lax.rsqrt(jnp.sum(total * total, axis=1, keepdims=True) + EPSILON)
    hid[0] = total
    hid[1] = jnp.broadcast_to(inv, (16, BOT))
    b_buf[p] = (total * inv).astype(BF16)

    def b_send(k, carry):
        pltpu.make_async_remote_copy(
            b_buf.at[p],
            b_buf.at[p],
            b_sem.at[0],
            b_sem.at[1],
            device_id=(i, (p + k) % 16),
            device_id_type=MESH,
        ).start()
        return carry

    lax.fori_loop(1, 16, b_send, 0)
    loads[8].wait()
    loads[9].wait()
    wait_bytes(b_buf.at[pl.ds(0, 15)], b_sem.at[1])
    units[0, 0, 0] = jnp.concatenate([b_buf[2 * k] for k in range(8)], axis=0)
    units[1, 0, 0] = jnp.concatenate([b_buf[2 * k + 1] for k in range(8)], axis=0)

    def neighbour(along_x, step):
        if along_x:
            return ((x + step) % SIDE) * SIDE + y
        return x * SIDE + (y + step) % SIDE

    def gather_copy(half, stage, forward):
        first = stage < 2
        along_x = (half == 0) == first
        step = 1 if forward else SIDE - 1
        base = 64 * half
        if stage % 2 == 0:
            src_slot, dst_slot, rows = 0, (3 if forward else 1), pl.ds(base, 64)
        else:
            src_slot, dst_slot = (3 if forward else 1), 2
            rows = pl.ds(base if forward else base + 32, 32)
        line = 0 if first else slice(None)

        def view(slot):
            if along_x:
                return units.at[c, slot, 0, rows] if first else units.at[c, slot, :, rows]
            return units.at[c, 0, slot, rows] if first else units.at[c, :, slot, rows]

        n = half * 8 + stage * 2 + (0 if forward else 1)
        return pltpu.make_async_remote_copy(
            view(src_slot),
            view(dst_slot),
            ag_send.at[n],
            ag_recv.at[n],
            device_id=(neighbour(along_x, step), p),
            device_id_type=MESH,
        )

    gather = [
        [[gather_copy(half, stage, forward) for forward in (True, False)] for stage in range(4)]
        for half in range(2)
    ]

    def gather_start(stage):
        for half in range(2):
            for copy in gather[half][stage]:
                copy.start()

    def gather_wait(stage):
        for half in range(2):
            for copy in gather[half][stage]:
                copy.wait_recv()

    def share_copy(half, second):
        rows = pl.ds(64 * half, 64)
        if half == 0:
            ref = units.at[c, :, pl.ds(1, 3), rows] if second else units.at[c, pl.ds(1, 3), 0, rows]
        else:
            ref = units.at[c, pl.ds(1, 3), :, rows] if second else units.at[c, 0, pl.ds(1, 3), rows]
        n = half * 2 + second
        return ref, pltpu.make_async_remote_copy(
            ref, ref, sh_send.at[n], sh_recv.at[n], device_id=(i, sibling), device_id_type=MESH
        )

    share = [[share_copy(half, second) for second in range(2)] for half in range(2)]

    gather_start(0)

    def logits(j, carry):
        top_s, top_t = carry
        columns = pl.ds(pl.multiple_of(j * TILE, TILE), TILE)
        logit_s = jnp.dot(units[0, 0, 0], ps[:, columns], preferred_element_type=F32) * STUDENT_SCALE
        ls_buf[:, columns] = logit_s
        raw_t = jnp.dot(units[1, 0, 0], pt[:, columns], preferred_element_type=F32)
        for q in range(TILE // 128):
            lanes = slice(128 * q, 128 * (q + 1))
            center = cen[pl.ds(j * (TILE // 128) + q, 1), :]
            logit_t = (raw_t[:, lanes] - center) * TEACHER_SCALE
            lt_buf[:, pl.ds(pl.multiple_of(j * TILE + 128 * q, 128), 128)] = logit_t
            top_s = jnp.maximum(top_s, logit_s[:, lanes])
            top_t = jnp.maximum(top_t, logit_t)
        return top_s, top_t

    low = jnp.full((ROWS, 128), -jnp.inf, F32)
    tops = lax.fori_loop(0, tiles, logits, (low, low))
    top_s = jnp.max(tops[0], axis=1, keepdims=True)
    top_t = jnp.max(tops[1], axis=1, keepdims=True)
    gather_wait(0)
    gather_start(1)

    def sums(j, carry):
        sum_s, sum_t, cross = carry
        for q in range(TILE // 128):
            columns = pl.ds(pl.multiple_of(j * TILE + 128 * q, 128), 128)
            logit_s = ls_buf[:, columns]
            exp_s = jnp.exp(logit_s - top_s)
            exp_t = jnp.exp(lt_buf[:, columns] - top_t)
            ls_buf[:, columns] = exp_s
            lt_buf[:, columns] = exp_t
            sum_s = sum_s + exp_s
            sum_t = sum_t + exp_t
            cross = cross + exp_t * logit_s
        return sum_s, sum_t, cross

    zero = jnp.zeros((ROWS, 128), F32)
    sum_s, sum_t, cross = lax.fori_loop(0, tiles, sums, (zero, zero, zero))
    lane = lax.broadcasted_iota(jnp.int32, (ROWS, 128), 1)
    table = jnp.where(lane == 0, top_s, jnp.where(lane == 1, top_t, 0.0))
    for n, value in ((2, sum_s), (3, sum_t), (4, cross)):
        table = jnp.where(lane == n, jnp.sum(value, axis=1, keepdims=True), table)
    st_buf[p] = table.T[:8]

    def c_send(k, carry):
        pltpu.make_async_remote_copy(
            st_buf.at[p],
            st_buf.at[p],
            c_sem.at[0],
            c_sem.at[1],
            device_id=(i, (p + k) % 16),
            device_id_type=MESH,
        ).start()
        return carry

    lax.fori_loop(1, 16, c_send, 0)
    gather_wait(1)
    gather_start(2)
    share[0][0][1].start()
    share[1][0][1].start()
    wait_bytes(st_buf.at[pl.ds(0, 15)], c_sem.at[1])
    all_top_s, all_top_t = st_buf[:, 0, :], st_buf[:, 1, :]
    max_s = jnp.max(all_top_s, axis=0, keepdims=True)
    max_t = jnp.max(all_top_t, axis=0, keepdims=True)
    scale_t = jnp.exp(all_top_t - max_t)
    total_s = jnp.sum(st_buf[:, 2, :] * jnp.exp(all_top_s - max_s), axis=0, keepdims=True)
    total_t = jnp.sum(st_buf[:, 3, :] * scale_t, axis=0, keepdims=True)
    total_x = jnp.sum(st_buf[:, 4, :] * scale_t, axis=0, keepdims=True)
    count = jnp.full((1, 128), cnt_ref[0], jnp.int32)
    live = lax.broadcasted_iota(jnp.int32, (1, 128), 1) < count
    weight = jnp.where(live, 1.0 / count.astype(F32), 0.0).astype(BF16).astype(F32)
    factor_s = GRAD_SCALE * weight / total_s
    factor_t = GRAD_SCALE * weight / total_t
    tot_buf[0] = jnp.concatenate(
        [max_s, factor_s, max_t, factor_t, jnp.zeros((4, 128), F32)], axis=0
    )

    def t_send(k, carry):
        dx, dy = k // SIDE, k % SIDE
        target = ((x + SIDE - dx) % SIDE) * SIDE + (y + SIDE - dy) % SIDE
        pltpu.make_async_remote_copy(
            tot_buf.at[0],
            tot_buf.at[k],
            t_sem.at[0],
            t_sem.at[1],
            device_id=(target, p),
            device_id_type=MESH,
        ).start()
        return carry

    lax.fori_loop(1, IMG, t_send, 0)
    loss_rows = -(total_x / total_t - max_s - jnp.log(total_s))
    loss_ref[0] = jnp.sum(weight * loss_rows)
    own = st_buf[p]
    near_s = factor_s * jnp.exp(own[0:1] - max_s)
    near_t = factor_t * jnp.exp(own[1:2] - max_t)
    near = jnp.concatenate([near_s, near_t, jnp.zeros((126, 128), F32)], axis=0).T
    near_s, near_t = near[:, 0:1], near[:, 1:2]

    def rows_gradient(j, carry):
        columns = pl.ds(pl.multiple_of(j * TILE, TILE), TILE)
        grad = (ls_buf[:, columns] * near_s - lt_buf[:, columns] * near_t).astype(BF16)
        return carry + lax.dot_general(
            grad, ps[:, columns], (((1,), (1,)), ((), ())), preferred_element_type=F32
        )

    d_src[...] = lax.fori_loop(0, tiles, rows_gradient, jnp.zeros((ROWS, BOT), F32)).reshape(
        8, 16, BOT
    )

    def d_send(k, carry):
        z2 = (z + k) % 8
        pltpu.make_async_remote_copy(
            d_src.at[z2],
            d_recv.at[p],
            d_sem.at[0],
            d_sem.at[1],
            device_id=(i, z2 * 2),
            device_id_type=MESH,
        ).start()
        return carry

    lax.fori_loop(1, 8, d_send, 0)

    @pl.when(c == 1)
    def _():
        d_send(0, 0)

    gather_wait(2)
    gather_start(3)
    gather_wait(3)
    share[0][1][1].start()
    share[1][1][1].start()

    @pl.when(c == 0)
    def _():
        d_recv[p] = d_src[z]
        wait_bytes(d_recv.at[pl.ds(0, 15)], d_sem.at[1])
        grad = d_recv[0]
        for k in range(1, 16):
            grad = grad + d_recv[k]
        hidden, inverse = hid[0], hid[1]
        inner = jnp.sum(hidden * grad, axis=1, keepdims=True)
        e_buf[z] = (
            grad * inverse - hidden * inner * (inverse * inverse * inverse)
        ).astype(BF16)

        def e_send(k, carry):
            pltpu.make_async_remote_copy(
                e_buf.at[z],
                e_buf.at[z],
                e_sem.at[0],
                e_sem.at[1],
                device_id=(i, (p + k) % 16),
                device_id_type=MESH,
            ).start()
            return carry

        lax.fori_loop(1, 16, e_send, 0)

    for half in range(2):
        for second in range(2):
            other = share[half][second][1]
            other.wait_recv()
    wait_bytes(tot_buf.at[pl.ds(1, 15)], t_sem.at[1])
    g_acc[...] = jnp.zeros_like(g_acc)

    def protos_gradient(k, carry):
        dx, dy = k // 2, (k % 2) * 2
        unit_s = units[0, dx, pl.ds(dy, 2)].reshape(2 * ROWS, BOT)
        unit_t = units[1, dx, pl.ds(dy, 2)].reshape(2 * ROWS, BOT)
        both = tot_buf[pl.ds(2 * k, 2)]
        wide = jnp.concatenate([both[0], both[1]], axis=1)
        for q in range(width // 128):
            block = pl.ds(128 * q, 128)
            contract = (((1,), (1,)), ((), ()))
            logit_s = (
                lax.dot_general(ps_own_t[block, :], unit_s, contract, preferred_element_type=F32)
                * STUDENT_SCALE
            )
            raw_t = lax.dot_general(pt_own_t[block, :], unit_t, contract, preferred_element_type=F32)
            center = cen_own_t[block, 0:1]
            logit_t = (raw_t - center) * TEACHER_SCALE
            grad = (
                jnp.exp(logit_s - wide[0:1]) * wide[1:2] - jnp.exp(logit_t - wide[2:3]) * wide[3:4]
            ).astype(BF16)
            g_acc[block, :] += jnp.dot(grad, unit_s, preferred_element_type=F32)
        return carry

    lax.fori_loop(0, IMG // 2, protos_gradient, 0)
    g_src[...] = g_acc[...].T.astype(BF16).reshape(IMG, 16, width)
    g_recv[i] = g_src[i]

    def g_send(k, carry):
        target = (i + k) % IMG
        pltpu.make_async_remote_copy(
            g_src.at[target],
            g_recv.at[i],
            g_sem.at[0],
            g_sem.at[1],
            device_id=(target, p),
            device_id_type=MESH,
        ).start()
        return carry

    lax.fori_loop(1, IMG, g_send, 0)

    @pl.when(c == 0)
    def _():
        wait_bytes(e_buf.at[pl.ds(0, 7)], e_sem.at[1])

    @pl.when(c == 1)
    def _():
        wait_bytes(e_buf, e_sem.at[1])

    grad_hidden = e_buf[...].reshape(ROWS, BOT)
    f_src[...] = (
        lax.dot_general(
            grad_hidden, rows_s[...], (((0,), (0,)), ((), ())), preferred_element_type=F32
        )
    ).reshape(IMG, 16, BOT)

    def f_send(k, carry):
        target = (i + k) % IMG
        pltpu.make_async_remote_copy(
            f_src.at[target],
            f_recv.at[i],
            f_sem.at[0],
            f_sem.at[1],
            device_id=(target, p),
            device_id_type=MESH,
        ).start()
        return carry

    lax.fori_loop(1, IMG, f_send, 0)
    f_recv[i] = f_src[i]

    wait_bytes(g_recv.at[pl.ds(0, 15)], g_sem.at[1])
    for k in range(IMG):
        gp_ref[:, width * k : width * (k + 1)] = g_recv[k].astype(F32)
    wait_bytes(f_recv.at[pl.ds(0, 15)], f_sem.at[1])
    bottleneck = f_recv[0]
    for k in range(1, IMG):
        bottleneck = bottleneck + f_recv[k]
    gb_ref[...] = bottleneck.T

    a1.wait_send()
    wait_bytes(a2_recv, a2_sem.at[0])
    wait_bytes(b_buf.at[pl.ds(0, 15)], b_sem.at[0])
    wait_bytes(st_buf.at[pl.ds(0, 15)], c_sem.at[0])
    wait_bytes(tot_buf.at[pl.ds(0, 15)], t_sem.at[0])
    wait_bytes(g_recv.at[pl.ds(0, 15)], g_sem.at[0])
    wait_bytes(f_recv.at[pl.ds(0, 15)], f_sem.at[0])

    @pl.when(c == 0)
    def _():
        wait_bytes(d_src.at[pl.ds(0, 7)], d_sem.at[0])
        wait_bytes(b_buf.at[pl.ds(0, 15)], e_sem.at[0])

    @pl.when(c == 1)
    def _():
        wait_bytes(d_src, d_sem.at[0])

    for half in range(2):
        for stage in range(4):
            for copy in gather[half][stage]:
                copy.wait_send()
        for second in range(2):
            share[half][second][1].wait_send()


def per_device(
    student_patch_tokens,
    teacher_patch_tokens,
    mask_counts,
    mask_index,
    student_bottleneck,
    teacher_bottleneck,
    student_protos,
    teacher_protos,
    center,
):
    patches, features = student_patch_tokens.shape[1:]
    protos = student_protos.shape[1]
    width = protos // IMG
    anywhere = pl.BlockSpec(memory_space=pl.ANY)
    dma = pltpu.SemaphoreType.DMA
    outs = pl.pallas_call(
        kernel,
        out_shape=(
            jax.ShapeDtypeStruct((1,), F32),
            jax.ShapeDtypeStruct((BOT // IMG, protos), F32),
            jax.ShapeDtypeStruct((features, BOT // IMG), F32),
        ),
        in_specs=[
            anywhere,
            anywhere,
            pl.BlockSpec(memory_space=pltpu.SMEM),
            anywhere,
            anywhere,
            anywhere,
            anywhere,
            anywhere,
            anywhere,
        ],
        out_specs=(
            pl.BlockSpec(memory_space=pltpu.SMEM),
            pl.BlockSpec(memory_space=pltpu.VMEM),
            pl.BlockSpec(memory_space=pltpu.VMEM),
        ),
        scratch_shapes=[
            pltpu.VMEM((patches, features), BF16),
            pltpu.VMEM((patches, features), BF16),
            pltpu.VMEM((1, ROWS), jnp.int32),
            pltpu.VMEM((features, BOT), BF16),
            pltpu.VMEM((features, BOT), BF16),
            pltpu.VMEM((BOT, protos), BF16),
            pltpu.VMEM((BOT, protos), BF16),
            pltpu.VMEM((protos // 128, 128), F32),
            pltpu.VMEM((BOT, width), BF16),
            pltpu.VMEM((BOT, width), BF16),
            pltpu.VMEM((ROWS, features), BF16),
            pltpu.VMEM((ROWS, BOT), F32),
            pltpu.VMEM((ROWS, BOT), F32),
            pltpu.VMEM((8, 16, BOT), F32),
            pltpu.VMEM((7, 16, BOT), F32),
            pltpu.VMEM((2, 16, BOT), F32),
            pltpu.VMEM((16, 16, BOT), BF16),
            pltpu.VMEM((2, SIDE, SIDE, ROWS, BOT), BF16),
            pltpu.VMEM((ROWS, protos), F32),
            pltpu.VMEM((ROWS, protos), F32),
            pltpu.VMEM((16, 8, 128), F32),
            pltpu.VMEM((IMG, 8, 128), F32),
            pltpu.VMEM((8, 16, BOT), F32),
            pltpu.VMEM((16, 16, BOT), F32),
            pltpu.VMEM((8, 16, BOT), BF16),
            pltpu.VMEM((width, BOT), BF16),
            pltpu.VMEM((width, BOT), BF16),
            pltpu.VMEM((width, 128), F32),
            pltpu.VMEM((width, BOT), F32),
            pltpu.VMEM((IMG, 16, width), BF16),
            pltpu.VMEM((IMG, 16, width), BF16),
            pltpu.VMEM((IMG, 16, features), F32),
            pltpu.VMEM((IMG, 16, features), F32),
            dma((10,)),
            dma((2,)),
            dma((2,)),
            dma((2,)),
            dma((2,)),
            dma((2,)),
            dma((2,)),
            dma((2,)),
            dma((2,)),
            dma((2,)),
            dma((16,)),
            dma((16,)),
            dma((4,)),
            dma((4,)),
        ],
        compiler_params=pltpu.CompilerParams(
            collective_id=0, has_side_effects=True, vmem_limit_bytes=56 * 1024 * 1024
        ),
    )(
        student_patch_tokens,
        teacher_patch_tokens,
        mask_counts,
        mask_index,
        student_bottleneck,
        teacher_bottleneck,
        student_protos,
        teacher_protos,
        center.reshape(protos // 128, 128),
    )
    return outs


def solution(mesh):
    placed = (
        P("img", None, "proto"),
        P("img", None, "proto"),
        P("img"),
        P("img", None),
        P("proto", None),
        P("proto", None),
        P(None, "proto"),
        P(None, "proto"),
        P("proto"),
    )
    return jax.shard_map(
        per_device,
        mesh=mesh,
        in_specs=placed,
        out_specs=(P("img"), P("img", "proto"), P("proto", "img")),
        check_vma=False,
    )
```

```python
import math

import jax
import jax.numpy as jnp
from jax import lax
from jax.experimental import pallas as pl
from jax.experimental.pallas import tpu as pltpu
from jax.sharding import PartitionSpec as P

EPSILON = 1e-06
STUDENT_SCALE = 10.0
LOG2E = 1.0 / math.log(2.0)
STUDENT_2 = 10.0 * LOG2E
TEACHER_2 = 25.0 * LOG2E
GRAD_SCALE = 40960.0
MESH = pl.DeviceIdType.MESH
F32 = jnp.float32
BF16 = jnp.bfloat16

SIDE = 4
IMG = 16
DEEP = 8
ROWS = 128
BOT = 256
TILE = 1024
CONTRACT_LAST = (((1,), (1,)), ((), ()))
CONTRACT_FIRST = (((0,), (0,)), ((), ()))

Z_STEPS = (4, 3, 5, 2, 6, 1, 7)
PLANE_STEPS = tuple(
    sorted(
        ((dx, dy) for dx in range(SIDE) for dy in range(SIDE) if dx or dy),
        key=lambda d: -(min(d[0], SIDE - d[0]) + min(d[1], SIDE - d[1])),
    )
)


def wait_bytes(ref, sem):
    pltpu.make_async_copy(ref, ref, sem).wait()


def columns_of(rows):
    pad = jnp.zeros((128 - rows.shape[0], 128), F32)
    return jnp.concatenate([rows, pad], axis=0).T


def kernel(
    tok_s_h,
    tok_t_h,
    cnt_h,
    idx_h,
    bs_h,
    bt_h,
    ps_h,
    pt_h,
    cen_h,
    gp_h,
    gb_ref,
    loss_ref,
    tok_s,
    tok_t,
    cnt,
    idx,
    bs,
    bt,
    ps,
    pt,
    cen,
    ps_own,
    pt_own,
    rows_s,
    a1_src,
    a1_recv,
    a2_src,
    a2_recv,
    hid,
    b_buf,
    units,
    ls_buf,
    lt_buf,
    p_src,
    p_recv,
    ps_st,
    st_buf,
    tot_buf,
    d_src,
    d_recv,
    d_col,
    h_buf,
    e_buf,
    ps_own_t,
    pt_own_t,
    cen_own_t,
    g_acc,
    g_src,
    f_src,
    f_recv,
    load_sem,
    a1_sem,
    a2_sem,
    hid_sem,
    b_sem,
    b2_sem,
    p_sem,
    pst_sem,
    c_sem,
    t_sem,
    d_sem,
    h_sem,
    e_sem,
    f_sem,
    g_sem,
    ag_send,
    ag_recv,
    sh_send,
    sh_recv,
):
    i = lax.axis_index("img")
    p = lax.axis_index("proto")
    x, y = i // SIDE, i % SIDE
    z, c = p // 2, p % 2
    width = ps_own.shape[1]
    tiles = ps.shape[1] // TILE
    sibling = p + 1 - 2 * c
    core_0 = c == 0

    def z_peer(step):
        return (i, ((z + step) % DEEP) * 2 + c)

    def plane_peer(dx, dy):
        return ((x + dx) % SIDE) * SIDE + (y + dy) % SIDE

    def remote(src, dst, sems, device):
        return pltpu.make_async_remote_copy(
            src, dst, sems.at[0], sems.at[1], device_id=device, device_id_type=MESH
        )

    barrier = pltpu.get_barrier_semaphore()
    pl.semaphore_signal(barrier, inc=1, device_id=(i, sibling), device_id_type=MESH)
    for step in Z_STEPS:
        pl.semaphore_signal(barrier, inc=1, device_id=z_peer(step), device_id_type=MESH)
    for dx, dy in PLANE_STEPS:
        pl.semaphore_signal(barrier, inc=1, device_id=(plane_peer(dx, dy), p), device_id_type=MESH)

    own_columns = pl.ds(pl.multiple_of(i * width, 128), width)
    loads = [
        pltpu.make_async_copy(src, dst, load_sem.at[n])
        for n, (src, dst) in enumerate(
            (
                (idx_h, idx),
                (tok_s_h.at[0], tok_s),
                (bs_h, bs),
                (tok_t_h.at[0], tok_t),
                (bt_h, bt),
                (cen_h, cen),
                (ps_h.at[:, own_columns], ps_own),
                (pt_h.at[:, own_columns], pt_own),
                (ps_h, ps),
                (pt_h, pt),
                (cnt_h, cnt),
            )
        )
    ]
    for load in loads[:5]:
        load.start()

    loads[0].wait()
    spread = jnp.broadcast_to(idx[...].astype(F32), (ROWS, ROWS)).T
    patch = lax.broadcasted_iota(jnp.int32, (ROWS, ROWS), 1).astype(F32)
    picker = jnp.concatenate(
        [(spread == patch).astype(F32), (spread == patch + 128.0).astype(F32)], axis=1
    ).astype(BF16)
    loads[1].wait()
    rows_s[...] = jnp.dot(picker, tok_s[...], preferred_element_type=F32).astype(BF16)
    loads[3].wait()
    rows_t = jnp.dot(picker, tok_t[...], preferred_element_type=F32).astype(BF16)
    loads[2].wait()
    part_s = jnp.dot(rows_s[...], bs[...], preferred_element_type=F32)
    loads[4].wait()
    part_t = jnp.dot(rows_t, bt[...], preferred_element_type=F32)
    a1_src[...] = jnp.where(core_0, part_t, part_s).reshape(DEEP, 16, BOT)
    a2_src[...] = jnp.where(core_0, part_s, part_t).reshape(DEEP, 16, BOT)

    pl.semaphore_wait(barrier, 1 + len(Z_STEPS) + len(PLANE_STEPS))

    a1 = remote(a1_src, a1_recv, a1_sem, (i, sibling))
    a1.start()
    for load in loads[5:]:
        load.start()
    a1.wait_recv()
    a2_src[...] = a2_src[...] + a1_recv[...]
    for step in Z_STEPS:
        remote(
            a2_src.at[(z + step) % DEEP], a2_recv.at[step - 1], a2_sem, z_peer(step)
        ).start()

    for load in loads[5:8]:
        load.wait()
    ps_own_t[...] = ps_own[...].astype(F32).T.astype(BF16)
    pt_own_t[...] = pt_own[...].astype(F32).T.astype(BF16)
    for q in range(width // 128):
        cen_own_t[pl.ds(128 * q, 128), :] = jnp.broadcast_to(
            cen[pl.ds(i * (width // 128) + q, 1), :], (128, 128)
        ).T

    wait_bytes(a2_recv, a2_sem.at[1])
    total = a2_src[z]
    for k in range(DEEP - 1):
        total = total + a2_recv[k]
    inv = lax.rsqrt(jnp.sum(total * total, axis=1, keepdims=True) + EPSILON)
    b_buf[c, z] = (total * inv).astype(BF16)

    for step in Z_STEPS:
        remote(b_buf.at[c, z], b_buf.at[c, z], b_sem, z_peer(step)).start()
    hid[c] = total
    hidden_copy = remote(hid.at[c], hid.at[c], hid_sem, (i, sibling))
    hidden_copy.start()
    for load in loads[8:]:
        load.wait()
    wait_bytes(b_buf.at[c, pl.ds(0, DEEP - 1)], b_sem.at[1])
    b2 = remote(b_buf.at[c], b_buf.at[c], b2_sem, (i, sibling))
    b2.start()
    b2.wait_recv()
    units[:, 0, 0] = b_buf[...].reshape(2, ROWS, BOT)

    def gather_copy(half, stage, forward):
        first = stage < 2
        along_x = (half == 0) == first
        step = 1 if forward else SIDE - 1
        base = 64 * half
        if stage % 2 == 0:
            src_slot, dst_slot, rows = 0, (3 if forward else 1), pl.ds(base, 64)
        else:
            src_slot, dst_slot = (3 if forward else 1), 2
            rows = pl.ds(base if forward else base + 32, 32)

        def view(slot):
            if along_x:
                return units.at[c, slot, 0, rows] if first else units.at[c, slot, :, rows]
            return units.at[c, 0, slot, rows] if first else units.at[c, :, slot, rows]

        n = half * 8 + stage * 2 + (0 if forward else 1)
        return pltpu.make_async_remote_copy(
            view(src_slot),
            view(dst_slot),
            ag_send.at[n],
            ag_recv.at[n],
            device_id=(plane_peer(step, 0) if along_x else plane_peer(0, step), p),
            device_id_type=MESH,
        )

    gather = [
        [[gather_copy(half, stage, forward) for forward in (True, False)] for stage in range(4)]
        for half in range(2)
    ]

    def gather_start(stage):
        for half in range(2):
            for copy in gather[half][stage]:
                copy.start()

    def gather_wait(stage):
        for half in range(2):
            for copy in gather[half][stage]:
                copy.wait_recv()

    def share_copy(half, second):
        rows = pl.ds(64 * half, 64)
        if half == 0:
            ref = units.at[c, :, pl.ds(1, 3), rows] if second else units.at[c, pl.ds(1, 3), 0, rows]
        else:
            ref = units.at[c, pl.ds(1, 3), :, rows] if second else units.at[c, 0, pl.ds(1, 3), rows]
        n = half * 2 + second
        return pltpu.make_async_remote_copy(
            ref, ref, sh_send.at[n], sh_recv.at[n], device_id=(i, sibling), device_id_type=MESH
        )

    share = [[share_copy(half, second) for second in range(2)] for half in range(2)]

    gather_start(0)

    def logits(j, carry):
        top_s, top_t = carry
        columns = pl.ds(pl.multiple_of(j * TILE, TILE), TILE)
        raw_s = jnp.dot(units[0, 0, 0], ps[:, columns], preferred_element_type=F32)
        raw_t = jnp.dot(units[1, 0, 0], pt[:, columns], preferred_element_type=F32)
        for q in range(TILE // 128):
            lanes = slice(128 * q, 128 * (q + 1))
            here = pl.ds(pl.multiple_of(j * TILE + 128 * q, 128), 128)
            ls_buf[:, here] = raw_s[:, lanes]
            moved = raw_t[:, lanes] - cen[pl.ds(j * (TILE // 128) + q, 1), :]
            lt_buf[:, here] = moved
            top_s = jnp.maximum(top_s, raw_s[:, lanes])
            top_t = jnp.maximum(top_t, moved)
        return top_s, top_t

    low = jnp.full((ROWS, 128), -jnp.inf, F32)
    tops = lax.fori_loop(0, tiles, logits, (low, low))
    top_s = jnp.max(tops[0], axis=1, keepdims=True)
    top_t = jnp.max(tops[1], axis=1, keepdims=True)
    gather_wait(0)
    gather_start(1)

    shift_s = top_s * STUDENT_2
    shift_t = top_t * TEACHER_2

    def sums(j, carry):
        sum_s, sum_t, cross, acc_s, acc_t = carry
        columns = pl.ds(pl.multiple_of(j * TILE, TILE), TILE)
        part_s, part_t = [], []
        for q in range(TILE // 128):
            here = pl.ds(pl.multiple_of(j * TILE + 128 * q, 128), 128)
            raw_s = ls_buf[:, here]
            exp_s = jnp.exp2(raw_s * STUDENT_2 - shift_s)
            exp_t = jnp.exp2(lt_buf[:, here] * TEACHER_2 - shift_t)
            sum_s = sum_s + exp_s
            sum_t = sum_t + exp_t
            cross = cross + exp_t * raw_s
            part_s.append(exp_s.astype(BF16))
            part_t.append(exp_t.astype(BF16))
        acc_s = acc_s + lax.dot_general(
            jnp.concatenate(part_s, axis=1), ps[:, columns], CONTRACT_LAST, preferred_element_type=F32
        )
        acc_t = acc_t + lax.dot_general(
            jnp.concatenate(part_t, axis=1), ps[:, columns], CONTRACT_LAST, preferred_element_type=F32
        )
        return sum_s, sum_t, cross, acc_s, acc_t

    zero = jnp.zeros((ROWS, 128), F32)
    wide = jnp.zeros((ROWS, BOT), F32)
    sum_s, sum_t, cross, acc_s, acc_t = lax.fori_loop(
        0, tiles, sums, (zero, zero, zero, wide, wide)
    )
    p_src[...] = jnp.where(core_0, acc_t, acc_s)
    pair = remote(p_src, p_recv, p_sem, (i, sibling))
    pair.start()
    lane = lax.broadcasted_iota(jnp.int32, (ROWS, 128), 1)
    table = jnp.where(lane == 0, top_s, jnp.where(lane == 1, top_t, 0.0))
    for n, value in ((2, sum_s), (3, sum_t), (4, cross)):
        table = jnp.where(lane == n, jnp.sum(value, axis=1, keepdims=True), table)
    mine = table.T[:8]
    ps_st[0] = mine
    pair_stats = remote(ps_st.at[0], ps_st.at[1], pst_sem, (i, sibling))
    pair_stats.start()

    pair_stats.wait_recv()
    other = ps_st[1]
    best = jnp.maximum(mine[0:2], other[0:2])
    base = jnp.concatenate(
        [jnp.full((1, 128), STUDENT_2, F32), jnp.full((1, 128), TEACHER_2, F32)], axis=0
    )
    scale_mine = jnp.exp2((mine[0:2] - best) * base)
    scale_other = jnp.exp2((other[0:2] - best) * base)
    st_buf[z] = jnp.concatenate(
        [
            best,
            mine[2:4] * scale_mine + other[2:4] * scale_other,
            mine[4:5] * scale_mine[1:2] + other[4:5] * scale_other[1:2],
            jnp.zeros((3, 128), F32),
        ],
        axis=0,
    )
    for step in Z_STEPS:
        remote(st_buf.at[z], st_buf.at[z], c_sem, z_peer(step)).start()
    own_scale = columns_of(
        jnp.where(
            core_0,
            jnp.concatenate([scale_mine[0:1], scale_other[0:1]], axis=0),
            jnp.concatenate([scale_mine[1:2], scale_other[1:2]], axis=0),
        )
    )

    kept = jnp.where(core_0, acc_s, acc_t) * own_scale[:, 0:1]
    pair.wait_recv()
    d_src[...] = (kept + p_recv[...] * own_scale[:, 1:2]).reshape(DEEP, 16, BOT)
    for step in Z_STEPS:
        remote(d_src.at[(z + step) % DEEP], d_recv.at[z], d_sem, z_peer(step)).start()
    d_recv[z] = d_src[z]
    loads_count = jnp.full((1, 128), cnt[0], jnp.int32)
    live = lax.broadcasted_iota(jnp.int32, (1, 128), 1) < loads_count
    weight = jnp.where(live, 1.0 / loads_count.astype(F32), 0.0).astype(BF16).astype(F32)

    gather_wait(1)
    gather_start(2)
    share[0][0].start()
    share[1][0].start()

    wait_bytes(st_buf.at[pl.ds(0, DEEP - 1)], c_sem.at[1])
    all_top_s, all_top_t = st_buf[:, 0, :], st_buf[:, 1, :]
    max_s = jnp.max(all_top_s, axis=0, keepdims=True)
    max_t = jnp.max(all_top_t, axis=0, keepdims=True)
    scale_s = jnp.exp2((all_top_s - max_s) * STUDENT_2)
    scale_t = jnp.exp2((all_top_t - max_t) * TEACHER_2)
    total_s = jnp.sum(st_buf[:, 2, :] * scale_s, axis=0, keepdims=True)
    total_t = jnp.sum(st_buf[:, 3, :] * scale_t, axis=0, keepdims=True)
    total_x = jnp.sum(st_buf[:, 4, :] * scale_t, axis=0, keepdims=True)
    factor_s = GRAD_SCALE * weight / total_s
    factor_t = GRAD_SCALE * weight / total_t
    tot_buf[0] = jnp.concatenate(
        [max_s * STUDENT_2, factor_s, max_t * TEACHER_2, factor_t, jnp.zeros((4, 128), F32)], axis=0
    )

    for dx, dy in PLANE_STEPS:
        slot = ((SIDE - dx) % SIDE) * SIDE + (SIDE - dy) % SIDE
        remote(tot_buf.at[0], tot_buf.at[slot], t_sem, (plane_peer(dx, dy), p)).start()
    d_col[...] = columns_of(jnp.where(core_0, scale_s * factor_s, scale_t * factor_t))
    loss_rows = -(
        STUDENT_SCALE * (total_x / total_t) - STUDENT_SCALE * max_s - jnp.log(total_s)
    )
    loss_ref[...] = weight * loss_rows

    wait_bytes(d_recv.at[pl.ds(0, DEEP - 1)], d_sem.at[1])
    scales = d_col[pl.ds(pl.multiple_of(16 * z, 16), 16), :]
    half_grad = d_recv[0] * scales[:, 0:1]
    for k in range(1, DEEP):
        half_grad = half_grad + d_recv[k] * scales[:, k : k + 1]
    h_buf[c] = half_grad
    h_copy = remote(h_buf.at[c], h_buf.at[c], h_sem, (i, sibling))
    h_copy.start()

    gather_wait(2)
    gather_start(3)

    hidden_copy.wait_recv()
    hidden = hid[0]
    inverse = lax.rsqrt(jnp.sum(hidden * hidden, axis=1, keepdims=True) + EPSILON)
    h_copy.wait_recv()
    grad = h_buf[0] - h_buf[1]
    inner = jnp.sum(hidden * grad, axis=1, keepdims=True)
    e_buf[z] = (grad * inverse - hidden * inner * (inverse * inverse * inverse)).astype(BF16)
    for step in Z_STEPS:
        remote(e_buf.at[z], e_buf.at[z], e_sem, z_peer(step)).start()

    gather_wait(3)
    share[0][1].start()
    share[1][1].start()

    for half in range(2):
        for second in range(2):
            share[half][second].wait_recv()
    wait_bytes(tot_buf.at[pl.ds(1, IMG - 1)], t_sem.at[1])
    g_acc[...] = jnp.zeros_like(g_acc)

    def protos_gradient(k, carry):
        dx, dy = k // 2, (k % 2) * 2
        unit_s = units[0, dx, pl.ds(dy, 2)].reshape(2 * ROWS, BOT)
        unit_t = units[1, dx, pl.ds(dy, 2)].reshape(2 * ROWS, BOT)
        both = tot_buf[pl.ds(2 * k, 2)]
        along = jnp.concatenate([both[0], both[1]], axis=1)
        for q in range(width // 128):
            block = pl.ds(128 * q, 128)
            raw_s = lax.dot_general(
                ps_own_t[block, :], unit_s, CONTRACT_LAST, preferred_element_type=F32
            )
            raw_t = lax.dot_general(
                pt_own_t[block, :], unit_t, CONTRACT_LAST, preferred_element_type=F32
            )
            exp_s = jnp.exp2(raw_s * STUDENT_2 - along[0:1])
            exp_t = jnp.exp2((raw_t - cen_own_t[block, 0:1]) * TEACHER_2 - along[2:3])
            slope = (exp_s * along[1:2] - exp_t * along[3:4]).astype(BF16)
            g_acc[block, :] += jnp.dot(slope, unit_s, preferred_element_type=F32)
        return carry

    lax.fori_loop(0, IMG // 2, protos_gradient, 0)
    g_src[...] = g_acc[...].T.astype(BF16).reshape(IMG, 16, width)
    for dx, dy in PLANE_STEPS:
        target = plane_peer(dx, dy)
        remote(g_src.at[target], gp_h.at[:, own_columns], g_sem, (target, p)).start()
    keep = pltpu.make_async_copy(g_src.at[i], gp_h.at[:, own_columns], load_sem.at[0])
    keep.start()

    wait_bytes(e_buf.at[pl.ds(0, DEEP - 1)], e_sem.at[1])
    grad_hidden = e_buf[...].reshape(ROWS, BOT)
    f_src[...] = (
        lax.dot_general(grad_hidden, rows_s[...], CONTRACT_FIRST, preferred_element_type=F32)
        .astype(BF16)
        .reshape(IMG, 16, BOT)
    )
    for dx, dy in PLANE_STEPS:
        target = plane_peer(dx, dy)
        remote(f_src.at[target], f_recv.at[i], f_sem, (target, p)).start()
    f_recv[i] = f_src[i]

    a1.wait_send()
    wait_bytes(a2_recv, a2_sem.at[0])
    hidden_copy.wait_send()
    wait_bytes(b_buf.at[c, pl.ds(0, DEEP - 1)], b_sem.at[0])
    b2.wait_send()
    pair.wait_send()
    pair_stats.wait_send()
    wait_bytes(st_buf.at[pl.ds(0, DEEP - 1)], c_sem.at[0])
    wait_bytes(d_recv.at[pl.ds(0, DEEP - 1)], d_sem.at[0])
    wait_bytes(tot_buf.at[pl.ds(1, IMG - 1)], t_sem.at[0])
    h_copy.wait_send()
    wait_bytes(e_buf.at[pl.ds(0, DEEP - 1)], e_sem.at[0])
    for half in range(2):
        for stage in range(4):
            for copy in gather[half][stage]:
                copy.wait_send()
        for second in range(2):
            share[half][second].wait_send()
    wait_bytes(g_src.at[pl.ds(0, IMG - 1)], g_sem.at[0])
    wait_bytes(f_src.at[pl.ds(0, IMG - 1)], f_sem.at[0])
    keep.wait()

    wait_bytes(f_recv.at[pl.ds(0, IMG - 1)], f_sem.at[1])
    bottleneck = f_recv[0].astype(F32)
    for k in range(1, IMG):
        bottleneck = bottleneck + f_recv[k].astype(F32)
    gb_ref[...] = bottleneck
    wait_bytes(gp_h.at[:, pl.ds(0, (IMG - 1) * width)], g_sem.at[1])


def finish(gp_in, gb_in, loss_in, loss_ref, gp_ref, gb_ref):
    gp_ref[...] = gp_in[...].astype(F32)
    gb_ref[...] = gb_in[...]
    loss_ref[0] = jnp.sum(loss_in[...])


def per_device(
    student_patch_tokens,
    teacher_patch_tokens,
    mask_counts,
    mask_index,
    student_bottleneck,
    teacher_bottleneck,
    student_protos,
    teacher_protos,
    center,
):
    patches, features = student_patch_tokens.shape[1:]
    protos = student_protos.shape[1]
    width = protos // IMG
    in_hbm = pl.BlockSpec(memory_space=pltpu.HBM)
    in_vmem = pl.BlockSpec(memory_space=pltpu.VMEM)
    dma = pltpu.SemaphoreType.DMA
    parts = pl.pallas_call(
        kernel,
        out_shape=(
            jax.ShapeDtypeStruct((BOT // IMG, protos), BF16),
            jax.ShapeDtypeStruct((BOT // IMG, features), F32),
            jax.ShapeDtypeStruct((1, 128), F32),
        ),
        in_specs=[in_hbm] * 9,
        out_specs=(in_hbm, in_vmem, in_vmem),
        scratch_shapes=[
            pltpu.VMEM((patches, features), BF16),
            pltpu.VMEM((patches, features), BF16),
            pltpu.SMEM((1,), jnp.int32),
            pltpu.VMEM((1, ROWS), jnp.int32),
            pltpu.VMEM((features, BOT), BF16),
            pltpu.VMEM((features, BOT), BF16),
            pltpu.VMEM((BOT, protos), BF16),
            pltpu.VMEM((BOT, protos), BF16),
            pltpu.VMEM((protos // 128, 128), F32),
            pltpu.VMEM((BOT, width), BF16),
            pltpu.VMEM((BOT, width), BF16),
            pltpu.VMEM((ROWS, features), BF16),
            pltpu.VMEM((DEEP, 16, BOT), F32),
            pltpu.VMEM((DEEP, 16, BOT), F32),
            pltpu.VMEM((DEEP, 16, BOT), F32),
            pltpu.VMEM((DEEP - 1, 16, BOT), F32),
            pltpu.VMEM((2, 16, BOT), F32),
            pltpu.VMEM((2, DEEP, 16, BOT), BF16),
            pltpu.VMEM((2, SIDE, SIDE, ROWS, BOT), BF16),
            pltpu.VMEM((ROWS, protos), F32),
            pltpu.VMEM((ROWS, protos), F32),
            pltpu.VMEM((ROWS, BOT), F32),
            pltpu.VMEM((ROWS, BOT), F32),
            pltpu.VMEM((2, 8, 128), F32),
            pltpu.VMEM((DEEP, 8, 128), F32),
            pltpu.VMEM((IMG, 8, 128), F32),
            pltpu.VMEM((DEEP, 16, BOT), F32),
            pltpu.VMEM((DEEP, 16, BOT), F32),
            pltpu.VMEM((ROWS, 128), F32),
            pltpu.VMEM((2, 16, BOT), F32),
            pltpu.VMEM((DEEP, 16, BOT), BF16),
            pltpu.VMEM((width, BOT), BF16),
            pltpu.VMEM((width, BOT), BF16),
            pltpu.VMEM((width, 128), F32),
            pltpu.VMEM((width, BOT), F32),
            pltpu.VMEM((IMG, 16, width), BF16),
            pltpu.VMEM((IMG, 16, features), BF16),
            pltpu.VMEM((IMG, 16, features), BF16),
            dma((11,)),
        ]
        + [dma((2,))] * 14
        + [
            dma((16,)),
            dma((16,)),
            dma((4,)),
            dma((4,)),
        ],
        compiler_params=pltpu.CompilerParams(
            collective_id=0, has_side_effects=True, vmem_limit_bytes=56 * 1024 * 1024
        ),
    )(
        student_patch_tokens,
        teacher_patch_tokens,
        mask_counts,
        mask_index,
        student_bottleneck,
        teacher_bottleneck,
        student_protos,
        teacher_protos,
        center.reshape(protos // 128, 128),
    )
    image_loss, grad_protos, grad_bottleneck = pl.pallas_call(
        finish,
        out_shape=(
            jax.ShapeDtypeStruct((1,), F32),
            jax.ShapeDtypeStruct((BOT // IMG, protos), F32),
            jax.ShapeDtypeStruct((BOT // IMG, features), F32),
        ),
        in_specs=[in_vmem] * 3,
        out_specs=(pl.BlockSpec(memory_space=pltpu.SMEM), in_vmem, in_vmem),
    )(*parts)
    return image_loss, grad_protos, grad_bottleneck.T


def solution(mesh):
    placed = (
        P("img", None, "proto"),
        P("img", None, "proto"),
        P("img"),
        P("img", None),
        P("proto", None),
        P("proto", None),
        P(None, "proto"),
        P(None, "proto"),
        P("proto"),
    )
    return jax.shard_map(
        per_device,
        mesh=mesh,
        in_specs=placed,
        out_specs=(P("img"), P("img", "proto"), P("proto", "img")),
        check_vma=False,
    )
```

```python
import math

import jax
import jax.numpy as jnp
from jax import lax
from jax.experimental import pallas as pl
from jax.experimental.pallas import tpu as pltpu
from jax.sharding import PartitionSpec as P

EPSILON = 1e-06
STUDENT_SCALE = 10.0
LOG2E = 1.0 / math.log(2.0)
STUDENT_2 = 10.0 * LOG2E
TEACHER_2 = 25.0 * LOG2E
GRAD_SCALE = 40960.0
MESH = pl.DeviceIdType.MESH
F32 = jnp.float32
BF16 = jnp.bfloat16

SIDE = 4
IMG = 16
DEEP = 8
ROWS = 128
BOT = 256
TILE = 1024
CONTRACT_LAST = (((1,), (1,)), ((), ()))
CONTRACT_FIRST = (((0,), (0,)), ((), ()))

Z_STEPS = (4, 3, 5, 2, 6, 1, 7)
PLANE_STEPS = tuple(
    sorted(
        ((dx, dy) for dx in range(SIDE) for dy in range(SIDE) if dx or dy),
        key=lambda d: -(min(d[0], SIDE - d[0]) + min(d[1], SIDE - d[1])),
    )
)


def wait_bytes(ref, sem):
    pltpu.make_async_copy(ref, ref, sem).wait()


def columns_of(rows):
    pad = jnp.zeros((128 - rows.shape[0], 128), F32)
    return jnp.concatenate([rows, pad], axis=0).T


def kernel(
    tok_s_h,
    tok_t_h,
    cnt_h,
    idx_h,
    bs_h,
    bt_h,
    ps_h,
    pt_h,
    cen_h,
    gp_h,
    gb_ref,
    loss_ref,
    tok_s,
    tok_t,
    cnt,
    idx,
    bs,
    bt,
    ps,
    pt,
    cen,
    ps_own,
    pt_own,
    rows_s,
    a1_src,
    a1_recv,
    a2_src,
    a2_recv,
    hid,
    b_buf,
    units,
    ls_buf,
    lt_buf,
    p_src,
    p_recv,
    ps_st,
    st_buf,
    tot_buf,
    d_src,
    d_recv,
    d_col,
    h_buf,
    e_buf,
    ps_own_t,
    pt_own_t,
    cen_own_t,
    g_acc,
    g_src,
    f_src,
    f_recv,
    load_sem,
    a1_sem,
    a2_sem,
    hid_sem,
    b_sem,
    b2_sem,
    p_sem,
    pst_sem,
    c_sem,
    t_sem,
    d_sem,
    h_sem,
    e_sem,
    f_sem,
    g_sem,
    ag_send,
    ag_recv,
    sh_send,
    sh_recv,
):
    i = lax.axis_index("img")
    p = lax.axis_index("proto")
    x, y = i // SIDE, i % SIDE
    z, c = p // 2, p % 2
    width = ps_own.shape[1]
    tiles = ps.shape[1] // TILE
    sibling = p + 1 - 2 * c
    core_0 = c == 0

    def z_peer(step):
        return (i, ((z + step) % DEEP) * 2 + c)

    def plane_peer(dx, dy):
        return ((x + dx) % SIDE) * SIDE + (y + dy) % SIDE

    def remote(src, dst, sems, device):
        return pltpu.make_async_remote_copy(
            src, dst, sems.at[0], sems.at[1], device_id=device, device_id_type=MESH
        )

    barrier = pltpu.get_barrier_semaphore()
    pl.semaphore_signal(barrier, inc=1, device_id=(i, sibling), device_id_type=MESH)
    for step in Z_STEPS:
        pl.semaphore_signal(barrier, inc=1, device_id=z_peer(step), device_id_type=MESH)
    for dx, dy in PLANE_STEPS:
        pl.semaphore_signal(barrier, inc=1, device_id=(plane_peer(dx, dy), p), device_id_type=MESH)

    own_columns = pl.ds(pl.multiple_of(i * width, 128), width)
    loads = [
        pltpu.make_async_copy(src, dst, load_sem.at[n])
        for n, (src, dst) in enumerate(
            (
                (idx_h, idx),
                (tok_s_h.at[0], tok_s),
                (bs_h, bs),
                (tok_t_h.at[0], tok_t),
                (bt_h, bt),
                (cen_h, cen),
                (ps_h.at[:, own_columns], ps_own),
                (pt_h.at[:, own_columns], pt_own),
                (ps_h, ps),
                (pt_h, pt),
                (cnt_h, cnt),
            )
        )
    ]
    for load in loads[:5]:
        load.start()

    loads[0].wait()
    spread = jnp.broadcast_to(idx[...].astype(F32), (ROWS, ROWS)).T
    patch = lax.broadcasted_iota(jnp.int32, (ROWS, ROWS), 1).astype(F32)
    picker = jnp.concatenate(
        [(spread == patch).astype(F32), (spread == patch + 128.0).astype(F32)], axis=1
    ).astype(BF16)
    loads[1].wait()
    rows_s[...] = jnp.dot(picker, tok_s[...], preferred_element_type=F32).astype(BF16)
    loads[3].wait()
    rows_t = jnp.dot(picker, tok_t[...], preferred_element_type=F32).astype(BF16)
    loads[2].wait()
    part_s = jnp.dot(rows_s[...], bs[...], preferred_element_type=F32)
    loads[4].wait()
    part_t = jnp.dot(rows_t, bt[...], preferred_element_type=F32)
    a1_src[...] = jnp.where(core_0, part_t, part_s).reshape(DEEP, 16, BOT)
    a2_src[...] = jnp.where(core_0, part_s, part_t).reshape(DEEP, 16, BOT)

    pl.semaphore_wait(barrier, 1 + len(Z_STEPS) + len(PLANE_STEPS))

    a1 = remote(a1_src, a1_recv, a1_sem, (i, sibling))
    a1.start()
    a1.wait_recv()
    a2_src[...] = a2_src[...] + a1_recv[...]
    for step in Z_STEPS:
        remote(
            a2_src.at[(z + step) % DEEP], a2_recv.at[step - 1], a2_sem, z_peer(step)
        ).start()

    for load in loads[5:]:
        load.start()
    for load in loads[5:8]:
        load.wait()
    ps_own_t[...] = ps_own[...].astype(F32).T.astype(BF16)
    pt_own_t[...] = pt_own[...].astype(F32).T.astype(BF16)
    for q in range(width // 128):
        cen_own_t[pl.ds(128 * q, 128), :] = jnp.broadcast_to(
            cen[pl.ds(i * (width // 128) + q, 1), :], (128, 128)
        ).T

    wait_bytes(a2_recv, a2_sem.at[1])
    total = a2_src[z]
    for k in range(DEEP - 1):
        total = total + a2_recv[k]
    inv = lax.rsqrt(jnp.sum(total * total, axis=1, keepdims=True) + EPSILON)
    b_buf[c, z] = (total * inv).astype(BF16)

    for step in Z_STEPS:
        remote(b_buf.at[c, z], b_buf.at[c, z], b_sem, z_peer(step)).start()
    hid[c] = total
    hidden_copy = remote(hid.at[c], hid.at[c], hid_sem, (i, sibling))
    hidden_copy.start()
    for load in loads[8:]:
        load.wait()
    wait_bytes(b_buf.at[c, pl.ds(0, DEEP - 1)], b_sem.at[1])
    b2 = remote(b_buf.at[c], b_buf.at[c], b2_sem, (i, sibling))
    b2.start()
    b2.wait_recv()
    units[:, 0, 0] = b_buf[...].reshape(2, ROWS, BOT)

    def gather_copy(half, stage, forward):
        first = stage < 2
        along_x = (half == 0) == first
        step = 1 if forward else SIDE - 1
        base = 64 * half
        if stage % 2 == 0:
            src_slot, dst_slot, rows = 0, (3 if forward else 1), pl.ds(base, 64)
        else:
            src_slot, dst_slot = (3 if forward else 1), 2
            rows = pl.ds(base if forward else base + 32, 32)

        def view(slot):
            if along_x:
                return units.at[c, slot, 0, rows] if first else units.at[c, slot, :, rows]
            return units.at[c, 0, slot, rows] if first else units.at[c, :, slot, rows]

        n = half * 8 + stage * 2 + (0 if forward else 1)
        return pltpu.make_async_remote_copy(
            view(src_slot),
            view(dst_slot),
            ag_send.at[n],
            ag_recv.at[n],
            device_id=(plane_peer(step, 0) if along_x else plane_peer(0, step), p),
            device_id_type=MESH,
        )

    gather = [
        [[gather_copy(half, stage, forward) for forward in (True, False)] for stage in range(4)]
        for half in range(2)
    ]

    def gather_start(stage):
        for half in range(2):
            for copy in gather[half][stage]:
                copy.start()

    def gather_wait(stage):
        for half in range(2):
            for copy in gather[half][stage]:
                copy.wait_recv()

    def share_copy(half, part):
        rows = pl.ds(64 * half, 64)
        if part == 0:
            ref = units.at[c, pl.ds(1, 3), 0, rows] if half == 0 else units.at[c, 0, pl.ds(1, 3), rows]
        else:
            slot = (1, 3, 2)[part - 1]
            ref = units.at[c, :, slot, rows] if half == 0 else units.at[c, slot, :, rows]
        n = half * 4 + part
        return pltpu.make_async_remote_copy(
            ref, ref, sh_send.at[n], sh_recv.at[n], device_id=(i, sibling), device_id_type=MESH
        )

    share = [[share_copy(half, part) for half in range(2)] for part in range(4)]

    def share_start(part):
        for copy in share[part]:
            copy.start()

    gather_start(0)

    def logits(j, carry):
        top_s, top_t = carry
        columns = pl.ds(pl.multiple_of(j * TILE, TILE), TILE)
        raw_s = jnp.dot(units[0, 0, 0], ps[:, columns], preferred_element_type=F32)
        raw_t = jnp.dot(units[1, 0, 0], pt[:, columns], preferred_element_type=F32)
        for q in range(TILE // 128):
            lanes = slice(128 * q, 128 * (q + 1))
            here = pl.ds(pl.multiple_of(j * TILE + 128 * q, 128), 128)
            ls_buf[:, here] = raw_s[:, lanes]
            moved = raw_t[:, lanes] - cen[pl.ds(j * (TILE // 128) + q, 1), :]
            lt_buf[:, here] = moved
            top_s = jnp.maximum(top_s, raw_s[:, lanes])
            top_t = jnp.maximum(top_t, moved)
        return top_s, top_t

    low = jnp.full((ROWS, 128), -jnp.inf, F32)
    tops = lax.fori_loop(0, tiles, logits, (low, low))
    top_s = jnp.max(tops[0], axis=1, keepdims=True)
    top_t = jnp.max(tops[1], axis=1, keepdims=True)

    shift_s = top_s * STUDENT_2
    shift_t = top_t * TEACHER_2

    def sums(j, carry):
        sum_s, sum_t, cross, acc_s, acc_t = carry
        columns = pl.ds(pl.multiple_of(j * TILE, TILE), TILE)
        part_s, part_t = [], []
        for q in range(TILE // 128):
            here = pl.ds(pl.multiple_of(j * TILE + 128 * q, 128), 128)
            raw_s = ls_buf[:, here]
            exp_s = jnp.exp2(raw_s * STUDENT_2 - shift_s)
            exp_t = jnp.exp2(lt_buf[:, here] * TEACHER_2 - shift_t)
            sum_s = sum_s + exp_s
            sum_t = sum_t + exp_t
            cross = cross + exp_t * raw_s
            part_s.append(exp_s.astype(BF16))
            part_t.append(exp_t.astype(BF16))
        acc_s = acc_s + lax.dot_general(
            jnp.concatenate(part_s, axis=1), ps[:, columns], CONTRACT_LAST, preferred_element_type=F32
        )
        acc_t = acc_t + lax.dot_general(
            jnp.concatenate(part_t, axis=1), ps[:, columns], CONTRACT_LAST, preferred_element_type=F32
        )
        return sum_s, sum_t, cross, acc_s, acc_t

    zero = jnp.zeros((ROWS, 128), F32)
    wide = jnp.zeros((ROWS, BOT), F32)
    state = lax.fori_loop(0, tiles // 3, sums, (zero, zero, zero, wide, wide))
    gather_wait(0)
    gather_start(1)
    sum_s, sum_t, cross, acc_s, acc_t = lax.fori_loop(tiles // 3, tiles, sums, state)
    p_src[...] = jnp.where(core_0, acc_t, acc_s)
    pair = remote(p_src, p_recv, p_sem, (i, sibling))
    pair.start()
    lane = lax.broadcasted_iota(jnp.int32, (ROWS, 128), 1)
    table = jnp.where(lane == 0, top_s, jnp.where(lane == 1, top_t, 0.0))
    for n, value in ((2, sum_s), (3, sum_t), (4, cross)):
        table = jnp.where(lane == n, jnp.sum(value, axis=1, keepdims=True), table)
    mine = table.T[:8]
    ps_st[0] = mine
    pair_stats = remote(ps_st.at[0], ps_st.at[1], pst_sem, (i, sibling))
    pair_stats.start()
    gather_wait(1)
    gather_start(2)
    share_start(0)

    pair_stats.wait_recv()
    other = ps_st[1]
    best = jnp.maximum(mine[0:2], other[0:2])
    base = jnp.concatenate(
        [jnp.full((1, 128), STUDENT_2, F32), jnp.full((1, 128), TEACHER_2, F32)], axis=0
    )
    scale_mine = jnp.exp2((mine[0:2] - best) * base)
    scale_other = jnp.exp2((other[0:2] - best) * base)
    st_buf[z] = jnp.concatenate(
        [
            best,
            mine[2:4] * scale_mine + other[2:4] * scale_other,
            mine[4:5] * scale_mine[1:2] + other[4:5] * scale_other[1:2],
            jnp.zeros((3, 128), F32),
        ],
        axis=0,
    )
    for step in Z_STEPS:
        remote(st_buf.at[z], st_buf.at[z], c_sem, z_peer(step)).start()
    own_scale = columns_of(
        jnp.where(
            core_0,
            jnp.concatenate([scale_mine[0:1], scale_other[0:1]], axis=0),
            jnp.concatenate([scale_mine[1:2], scale_other[1:2]], axis=0),
        )
    )

    kept = jnp.where(core_0, acc_s, acc_t) * own_scale[:, 0:1]
    pair.wait_recv()
    d_src[...] = (kept + p_recv[...] * own_scale[:, 1:2]).reshape(DEEP, 16, BOT)
    for step in Z_STEPS:
        remote(d_src.at[(z + step) % DEEP], d_recv.at[z], d_sem, z_peer(step)).start()
    d_recv[z] = d_src[z]
    count = jnp.full((1, 128), cnt[0, 0], jnp.int32)
    live = lax.broadcasted_iota(jnp.int32, (1, 128), 1) < count
    weight = jnp.where(live, 1.0 / count.astype(F32), 0.0).astype(BF16).astype(F32)

    gather_wait(2)
    gather_start(3)
    share_start(1)
    share_start(2)

    wait_bytes(st_buf.at[pl.ds(0, DEEP - 1)], c_sem.at[1])
    all_top_s, all_top_t = st_buf[:, 0, :], st_buf[:, 1, :]
    max_s = jnp.max(all_top_s, axis=0, keepdims=True)
    max_t = jnp.max(all_top_t, axis=0, keepdims=True)
    scale_s = jnp.exp2((all_top_s - max_s) * STUDENT_2)
    scale_t = jnp.exp2((all_top_t - max_t) * TEACHER_2)
    total_s = jnp.sum(st_buf[:, 2, :] * scale_s, axis=0, keepdims=True)
    total_t = jnp.sum(st_buf[:, 3, :] * scale_t, axis=0, keepdims=True)
    total_x = jnp.sum(st_buf[:, 4, :] * scale_t, axis=0, keepdims=True)
    factor_s = GRAD_SCALE * weight / total_s
    factor_t = GRAD_SCALE * weight / total_t
    tot_buf[0] = jnp.concatenate(
        [max_s * STUDENT_2, factor_s, max_t * TEACHER_2, factor_t, jnp.zeros((4, 128), F32)], axis=0
    )

    for dx, dy in PLANE_STEPS:
        slot = ((SIDE - dx) % SIDE) * SIDE + (SIDE - dy) % SIDE
        remote(tot_buf.at[0], tot_buf.at[slot], t_sem, (plane_peer(dx, dy), p)).start()
    d_col[...] = columns_of(jnp.where(core_0, scale_s * factor_s, scale_t * factor_t))
    loss_rows = -(
        STUDENT_SCALE * (total_x / total_t) - STUDENT_SCALE * max_s - jnp.log(total_s)
    )
    loss_ref[...] = weight * loss_rows

    wait_bytes(d_recv.at[pl.ds(0, DEEP - 1)], d_sem.at[1])
    scales = d_col[pl.ds(pl.multiple_of(16 * z, 16), 16), :]
    half_grad = d_recv[0] * scales[:, 0:1]
    for k in range(1, DEEP):
        half_grad = half_grad + d_recv[k] * scales[:, k : k + 1]
    h_buf[c] = half_grad
    h_copy = remote(h_buf.at[c], h_buf.at[c], h_sem, (i, sibling))
    h_copy.start()

    gather_wait(3)
    share_start(3)

    hidden_copy.wait_recv()
    hidden = hid[0]
    inverse = lax.rsqrt(jnp.sum(hidden * hidden, axis=1, keepdims=True) + EPSILON)
    h_copy.wait_recv()
    grad = h_buf[0] - h_buf[1]
    inner = jnp.sum(hidden * grad, axis=1, keepdims=True)
    e_buf[z] = (grad * inverse - hidden * inner * (inverse * inverse * inverse)).astype(BF16)
    for step in Z_STEPS:
        remote(e_buf.at[z], e_buf.at[z], e_sem, z_peer(step)).start()

    for part in share:
        for copy in part:
            copy.wait_recv()
    wait_bytes(tot_buf.at[pl.ds(1, IMG - 1)], t_sem.at[1])
    g_acc[...] = jnp.zeros_like(g_acc)

    def protos_gradient(dx, carry):
        unit_s = units[0, dx].reshape(SIDE * ROWS, BOT)
        unit_t = units[1, dx].reshape(SIDE * ROWS, BOT)
        raw_s = lax.dot_general(ps_own_t[...], unit_s, CONTRACT_LAST, preferred_element_type=F32)
        raw_t = lax.dot_general(pt_own_t[...], unit_t, CONTRACT_LAST, preferred_element_type=F32)
        totals = tot_buf[pl.ds(SIDE * dx, SIDE)]
        slopes = []
        for q in range(width // 128):
            block = slice(128 * q, 128 * (q + 1))
            center = cen_own_t[block, :]
            line = []
            for dy in range(SIDE):
                lanes = slice(128 * dy, 128 * (dy + 1))
                exp_s = jnp.exp2(raw_s[block, lanes] * STUDENT_2 - totals[dy, 0:1])
                exp_t = jnp.exp2((raw_t[block, lanes] - center) * TEACHER_2 - totals[dy, 2:3])
                line.append((exp_s * totals[dy, 1:2] - exp_t * totals[dy, 3:4]).astype(BF16))
            slopes.append(jnp.concatenate(line, axis=1))
        g_acc[...] += jnp.dot(
            jnp.concatenate(slopes, axis=0), unit_s, preferred_element_type=F32
        )
        return carry

    lax.fori_loop(0, SIDE, protos_gradient, 0)
    g_src[...] = g_acc[...].T.astype(BF16).reshape(IMG, 16, width)
    for dx, dy in PLANE_STEPS:
        target = plane_peer(dx, dy)
        remote(g_src.at[target], gp_h.at[:, own_columns], g_sem, (target, p)).start()
    keep = pltpu.make_async_copy(g_src.at[i], gp_h.at[:, own_columns], load_sem.at[0])
    keep.start()

    wait_bytes(e_buf.at[pl.ds(0, DEEP - 1)], e_sem.at[1])
    grad_hidden = e_buf[...].reshape(ROWS, BOT)
    f_src[...] = (
        lax.dot_general(grad_hidden, rows_s[...], CONTRACT_FIRST, preferred_element_type=F32)
        .astype(BF16)
        .reshape(IMG, 16, BOT)
    )
    for dx, dy in PLANE_STEPS:
        target = plane_peer(dx, dy)
        remote(f_src.at[target], f_recv.at[i], f_sem, (target, p)).start()
    f_recv[i] = f_src[i]

    a1.wait_send()
    wait_bytes(a2_recv, a2_sem.at[0])
    hidden_copy.wait_send()
    wait_bytes(b_buf.at[c, pl.ds(0, DEEP - 1)], b_sem.at[0])
    b2.wait_send()
    pair.wait_send()
    pair_stats.wait_send()
    wait_bytes(st_buf.at[pl.ds(0, DEEP - 1)], c_sem.at[0])
    wait_bytes(d_recv.at[pl.ds(0, DEEP - 1)], d_sem.at[0])
    wait_bytes(tot_buf.at[pl.ds(1, IMG - 1)], t_sem.at[0])
    h_copy.wait_send()
    wait_bytes(e_buf.at[pl.ds(0, DEEP - 1)], e_sem.at[0])
    for half in range(2):
        for stage in range(4):
            for copy in gather[half][stage]:
                copy.wait_send()
    for part in share:
        for copy in part:
            copy.wait_send()
    wait_bytes(g_src.at[pl.ds(0, IMG - 1)], g_sem.at[0])
    wait_bytes(f_src.at[pl.ds(0, IMG - 1)], f_sem.at[0])
    keep.wait()

    wait_bytes(f_recv.at[pl.ds(0, IMG - 1)], f_sem.at[1])
    bottleneck = f_recv[0].astype(F32)
    for k in range(1, IMG):
        bottleneck = bottleneck + f_recv[k].astype(F32)
    gb_ref[...] = bottleneck
    wait_bytes(gp_h.at[:, pl.ds(0, (IMG - 1) * width)], g_sem.at[1])


def finish(gp_in, gb_in, loss_in, loss_ref, gp_ref, gb_ref):
    gp_ref[...] = gp_in[...].astype(F32)
    gb_ref[...] = gb_in[...]
    loss_ref[0] = jnp.sum(loss_in[...])


def per_device(
    student_patch_tokens,
    teacher_patch_tokens,
    mask_counts,
    mask_index,
    student_bottleneck,
    teacher_bottleneck,
    student_protos,
    teacher_protos,
    center,
):
    patches, features = student_patch_tokens.shape[1:]
    protos = student_protos.shape[1]
    width = protos // IMG
    in_hbm = pl.BlockSpec(memory_space=pltpu.HBM)
    in_vmem = pl.BlockSpec(memory_space=pltpu.VMEM)
    dma = pltpu.SemaphoreType.DMA
    parts = pl.pallas_call(
        kernel,
        out_shape=(
            jax.ShapeDtypeStruct((BOT // IMG, protos), BF16),
            jax.ShapeDtypeStruct((BOT // IMG, features), F32),
            jax.ShapeDtypeStruct((1, 128), F32),
        ),
        in_specs=[in_hbm] * 9,
        out_specs=(in_hbm, in_vmem, in_vmem),
        scratch_shapes=[
            pltpu.VMEM((patches, features), BF16),
            pltpu.VMEM((patches, features), BF16),
            pltpu.SMEM((1, 1), jnp.int32),
            pltpu.VMEM((1, ROWS), jnp.int32),
            pltpu.VMEM((features, BOT), BF16),
            pltpu.VMEM((features, BOT), BF16),
            pltpu.VMEM((BOT, protos), BF16),
            pltpu.VMEM((BOT, protos), BF16),
            pltpu.VMEM((protos // 128, 128), F32),
            pltpu.VMEM((BOT, width), BF16),
            pltpu.VMEM((BOT, width), BF16),
            pltpu.VMEM((ROWS, features), BF16),
            pltpu.VMEM((DEEP, 16, BOT), F32),
            pltpu.VMEM((DEEP, 16, BOT), F32),
            pltpu.VMEM((DEEP, 16, BOT), F32),
            pltpu.VMEM((DEEP - 1, 16, BOT), F32),
            pltpu.VMEM((2, 16, BOT), F32),
            pltpu.VMEM((2, DEEP, 16, BOT), BF16),
            pltpu.VMEM((2, SIDE, SIDE, ROWS, BOT), BF16),
            pltpu.VMEM((ROWS, protos), F32),
            pltpu.VMEM((ROWS, protos), F32),
            pltpu.VMEM((ROWS, BOT), F32),
            pltpu.VMEM((ROWS, BOT), F32),
            pltpu.VMEM((2, 8, 128), F32),
            pltpu.VMEM((DEEP, 8, 128), F32),
            pltpu.VMEM((IMG, 8, 128), F32),
            pltpu.VMEM((DEEP, 16, BOT), F32),
            pltpu.VMEM((DEEP, 16, BOT), F32),
            pltpu.VMEM((ROWS, 128), F32),
            pltpu.VMEM((2, 16, BOT), F32),
            pltpu.VMEM((DEEP, 16, BOT), BF16),
            pltpu.VMEM((width, BOT), BF16),
            pltpu.VMEM((width, BOT), BF16),
            pltpu.VMEM((width, 128), F32),
            pltpu.VMEM((width, BOT), F32),
            pltpu.VMEM((IMG, 16, width), BF16),
            pltpu.VMEM((IMG, 16, features), BF16),
            pltpu.VMEM((IMG, 16, features), BF16),
            dma((11,)),
        ]
        + [dma((2,))] * 14
        + [
            dma((16,)),
            dma((16,)),
            dma((8,)),
            dma((8,)),
        ],
        compiler_params=pltpu.CompilerParams(
            collective_id=0, has_side_effects=True, vmem_limit_bytes=56 * 1024 * 1024
        ),
    )(
        student_patch_tokens,
        teacher_patch_tokens,
        mask_counts.reshape(1, 1),
        mask_index,
        student_bottleneck,
        teacher_bottleneck,
        student_protos,
        teacher_protos,
        center.reshape(protos // 128, 128),
    )
    image_loss, grad_protos, grad_bottleneck = pl.pallas_call(
        finish,
        out_shape=(
            jax.ShapeDtypeStruct((1,), F32),
            jax.ShapeDtypeStruct((BOT // IMG, protos), F32),
            jax.ShapeDtypeStruct((BOT // IMG, features), F32),
        ),
        in_specs=[in_vmem] * 3,
        out_specs=(pl.BlockSpec(memory_space=pltpu.SMEM), in_vmem, in_vmem),
    )(*parts)
    return image_loss, grad_protos, grad_bottleneck.T


def solution(mesh):
    placed = (
        P("img", None, "proto"),
        P("img", None, "proto"),
        P("img"),
        P("img", None),
        P("proto", None),
        P("proto", None),
        P(None, "proto"),
        P(None, "proto"),
        P("proto"),
    )
    return jax.shard_map(
        per_device,
        mesh=mesh,
        in_specs=placed,
        out_specs=(P("img"), P("img", "proto"), P("proto", "img")),
        check_vma=False,
    )
```

```python
import math

import jax
import jax.numpy as jnp
from jax import lax
from jax.experimental import pallas as pl
from jax.experimental.pallas import tpu as pltpu
from jax.sharding import PartitionSpec as P

EPSILON = 1e-06
STUDENT_SCALE = 10.0
LOG2E = 1.0 / math.log(2.0)
STUDENT_2 = 10.0 * LOG2E
TEACHER_2 = 25.0 * LOG2E
GRAD_SCALE = 40960.0
MESH = pl.DeviceIdType.MESH
F32 = jnp.float32
BF16 = jnp.bfloat16

SIDE = 4
IMG = 16
DEEP = 8
ROWS = 128
BOT = 256
TILE = 1024
CONTRACT_LAST = (((1,), (1,)), ((), ()))
CONTRACT_FIRST = (((0,), (0,)), ((), ()))

Z_STEPS = (4, 3, 5, 2, 6, 1, 7)
PLANE_STEPS = tuple(
    sorted(
        ((dx, dy) for dx in range(SIDE) for dy in range(SIDE) if dx or dy),
        key=lambda d: -(min(d[0], SIDE - d[0]) + min(d[1], SIDE - d[1])),
    )
)


def wait_bytes(ref, sem):
    pltpu.make_async_copy(ref, ref, sem).wait()


def columns_of(rows):
    pad = jnp.zeros((128 - rows.shape[0], 128), F32)
    return jnp.concatenate([rows, pad], axis=0).T


def kernel(
    tok_s_h,
    tok_t_h,
    cnt_h,
    idx_h,
    bs_h,
    bt_h,
    ps_h,
    pt_h,
    cen_h,
    gp_h,
    gb_ref,
    loss_ref,
    tok_s,
    tok_t,
    cnt,
    idx,
    bs,
    bt,
    pro,
    cen,
    ps_own,
    pt_own,
    rows_s,
    a1_src,
    a1_recv,
    a2_src,
    a2_recv,
    hid,
    b_buf,
    units,
    raw,
    p_src,
    p_recv,
    o_st,
    c_st,
    st_buf,
    tot_buf,
    d_src,
    d_recv,
    d_col,
    h_buf,
    e_buf,
    ps_own_t,
    pt_own_t,
    cen_own_t,
    g_acc,
    g_src,
    f_src,
    f_recv,
    load_sem,
    a1_sem,
    a2_sem,
    hid_sem,
    b_sem,
    b2_sem,
    p_sem,
    ost_sem,
    cst_sem,
    c_sem,
    t_sem,
    d_sem,
    h_sem,
    e_sem,
    f_sem,
    g_sem,
    ag_send,
    ag_recv,
    sh_send,
    sh_recv,
):
    i = lax.axis_index("img")
    p = lax.axis_index("proto")
    x, y = i // SIDE, i % SIDE
    z, c = p // 2, p % 2
    width = ps_own.shape[1]
    tiles = pro.shape[2] // TILE
    sibling = p + 1 - 2 * c
    core_0 = c == 0
    o = 1 - c
    base_c = jnp.where(core_0, STUDENT_2, TEACHER_2)
    base_o = jnp.where(core_0, TEACHER_2, STUDENT_2)

    def z_peer(step):
        return (i, ((z + step) % DEEP) * 2 + c)

    def plane_peer(dx, dy):
        return ((x + dx) % SIDE) * SIDE + (y + dy) % SIDE

    def remote(src, dst, sems, device):
        return pltpu.make_async_remote_copy(
            src, dst, sems.at[0], sems.at[1], device_id=device, device_id_type=MESH
        )

    barrier = pltpu.get_barrier_semaphore()
    pl.semaphore_signal(barrier, inc=1, device_id=(i, sibling), device_id_type=MESH)
    for step in Z_STEPS:
        pl.semaphore_signal(barrier, inc=1, device_id=z_peer(step), device_id_type=MESH)
    for dx, dy in PLANE_STEPS:
        pl.semaphore_signal(barrier, inc=1, device_id=(plane_peer(dx, dy), p), device_id_type=MESH)

    own_columns = pl.ds(pl.multiple_of(i * width, 128), width)
    loads = [
        pltpu.make_async_copy(src, dst, load_sem.at[n])
        for n, (src, dst) in enumerate(
            (
                (idx_h, idx),
                (tok_s_h.at[0], tok_s),
                (bs_h, bs),
                (tok_t_h.at[0], tok_t),
                (bt_h, bt),
                (cen_h, cen.at[1]),
                (ps_h.at[:, own_columns], ps_own),
                (pt_h.at[:, own_columns], pt_own),
                (ps_h, pro.at[0]),
                (pt_h, pro.at[1]),
                (cnt_h, cnt),
            )
        )
    ]
    for load in loads[:5]:
        load.start()

    loads[0].wait()
    spread = jnp.broadcast_to(idx[...].astype(F32), (ROWS, ROWS)).T
    patch = lax.broadcasted_iota(jnp.int32, (ROWS, ROWS), 1).astype(F32)
    picker = jnp.concatenate(
        [(spread == patch).astype(F32), (spread == patch + 128.0).astype(F32)], axis=1
    ).astype(BF16)
    loads[1].wait()
    rows_s[...] = jnp.dot(picker, tok_s[...], preferred_element_type=F32).astype(BF16)
    loads[3].wait()
    rows_t = jnp.dot(picker, tok_t[...], preferred_element_type=F32).astype(BF16)
    loads[2].wait()
    part_s = jnp.dot(rows_s[...], bs[...], preferred_element_type=F32)
    loads[4].wait()
    part_t = jnp.dot(rows_t, bt[...], preferred_element_type=F32)
    a1_src[...] = jnp.where(core_0, part_t, part_s).reshape(DEEP, 16, BOT)
    a2_src[...] = jnp.where(core_0, part_s, part_t).reshape(DEEP, 16, BOT)

    pl.semaphore_wait(barrier, 1 + len(Z_STEPS) + len(PLANE_STEPS))

    a1 = remote(a1_src, a1_recv, a1_sem, (i, sibling))
    a1.start()
    a1.wait_recv()
    a2_src[...] = a2_src[...] + a1_recv[...]
    for step in Z_STEPS:
        remote(
            a2_src.at[(z + step) % DEEP], a2_recv.at[step - 1], a2_sem, z_peer(step)
        ).start()

    cen[0] = jnp.zeros_like(cen[0])
    for load in loads[5:]:
        load.start()
    for load in loads[5:8]:
        load.wait()
    ps_own_t[...] = ps_own[...].astype(F32).T.astype(BF16)
    pt_own_t[...] = pt_own[...].astype(F32).T.astype(BF16)
    for q in range(width // 128):
        cen_own_t[pl.ds(128 * q, 128), :] = jnp.broadcast_to(
            cen[1, pl.ds(i * (width // 128) + q, 1), :], (128, 128)
        ).T

    wait_bytes(a2_recv, a2_sem.at[1])
    total = a2_src[z]
    for k in range(DEEP - 1):
        total = total + a2_recv[k]
    inv = lax.rsqrt(jnp.sum(total * total, axis=1, keepdims=True) + EPSILON)
    b_buf[c, z] = (total * inv).astype(BF16)

    for step in Z_STEPS:
        remote(b_buf.at[c, z], b_buf.at[c, z], b_sem, z_peer(step)).start()
    hid[c] = total
    hidden_copy = remote(hid.at[c], hid.at[c], hid_sem, (i, sibling))
    hidden_copy.start()
    for load in loads[8:]:
        load.wait()
    wait_bytes(b_buf.at[c, pl.ds(0, DEEP - 1)], b_sem.at[1])
    b2 = remote(b_buf.at[c], b_buf.at[c], b2_sem, (i, sibling))
    b2.start()
    units[c, 0, 0] = b_buf[c].reshape(ROWS, BOT)

    def gather_copy(half, stage, forward):
        first = stage < 2
        along_x = (half == 0) == first
        step = 1 if forward else SIDE - 1
        base = 64 * half
        if stage % 2 == 0:
            src_slot, dst_slot, rows = 0, (3 if forward else 1), pl.ds(base, 64)
        else:
            src_slot, dst_slot = (3 if forward else 1), 2
            rows = pl.ds(base if forward else base + 32, 32)

        def view(slot):
            if along_x:
                return units.at[c, slot, 0, rows] if first else units.at[c, slot, :, rows]
            return units.at[c, 0, slot, rows] if first else units.at[c, :, slot, rows]

        n = half * 8 + stage * 2 + (0 if forward else 1)
        return pltpu.make_async_remote_copy(
            view(src_slot),
            view(dst_slot),
            ag_send.at[n],
            ag_recv.at[n],
            device_id=(plane_peer(step, 0) if along_x else plane_peer(0, step), p),
            device_id_type=MESH,
        )

    gather = [
        [[gather_copy(half, stage, forward) for forward in (True, False)] for stage in range(4)]
        for half in range(2)
    ]

    def gather_start(stage):
        for half in range(2):
            for copy in gather[half][stage]:
                copy.start()

    def gather_wait(stage):
        for half in range(2):
            for copy in gather[half][stage]:
                copy.wait_recv()

    def share_copy(half, part):
        rows = pl.ds(64 * half, 64)
        if part == 0:
            ref = units.at[c, pl.ds(1, 3), 0, rows] if half == 0 else units.at[c, 0, pl.ds(1, 3), rows]
        else:
            slot = (1, 3, 2)[part - 1]
            ref = units.at[c, :, slot, rows] if half == 0 else units.at[c, slot, :, rows]
        n = half * 4 + part
        return pltpu.make_async_remote_copy(
            ref, ref, sh_send.at[n], sh_recv.at[n], device_id=(i, sibling), device_id_type=MESH
        )

    share = [[share_copy(half, part) for half in range(2)] for part in range(4)]

    def share_start(part):
        for copy in share[part]:
            copy.start()

    gather_start(0)

    def logits(kind):
        def step(j, top):
            columns = pl.ds(pl.multiple_of(j * TILE, TILE), TILE)
            product = jnp.dot(units[kind, 0, 0], pro[kind, :, columns], preferred_element_type=F32)
            for q in range(TILE // 128):
                moved = product[:, 128 * q : 128 * (q + 1)] - cen[
                    kind, pl.ds(j * (TILE // 128) + q, 1), :
                ]
                raw[kind, :, pl.ds(pl.multiple_of(j * TILE + 128 * q, 128), 128)] = moved
                top = jnp.maximum(top, moved)
            return top

        top = lax.fori_loop(0, tiles, step, jnp.full((ROWS, 128), -jnp.inf, F32), unroll=True)
        return jnp.max(top, axis=1, keepdims=True)

    top_c = logits(c)
    b2.wait_recv()
    units[o, 0, 0] = b_buf[o].reshape(ROWS, BOT)
    top_o = logits(o)

    def sums(kind, top, base):
        shift = top * base

        def step(j, carry):
            total, cross, acc = carry
            parts = []
            for q in range(TILE // 128):
                here = pl.ds(pl.multiple_of(j * TILE + 128 * q, 128), 128)
                power = jnp.exp2(raw[kind, :, here] * base - shift)
                total = total + power
                cross = cross + power * raw[1 - kind, :, here]
                parts.append(power.astype(BF16))
            columns = pl.ds(pl.multiple_of(j * TILE, TILE), TILE)
            acc = acc + lax.dot_general(
                jnp.concatenate(parts, axis=1),
                pro[0, :, columns],
                CONTRACT_LAST,
                preferred_element_type=F32,
            )
            return total, cross, acc

        zero = jnp.zeros((ROWS, 128), F32)
        total, cross, acc = lax.fori_loop(
            0, tiles, step, (zero, zero, jnp.zeros((ROWS, BOT), F32)), unroll=True
        )
        return total, cross, acc

    def statistics(top, total, cross):
        lane = lax.broadcasted_iota(jnp.int32, (ROWS, 128), 1)
        table = jnp.where(lane == 0, top, 0.0)
        for n, value in ((1, total), (2, cross)):
            table = jnp.where(lane == n, jnp.sum(value, axis=1, keepdims=True), table)
        return table.T[:8]

    total_o, cross_o, acc_o = sums(o, top_o, base_o)
    p_src[...] = acc_o
    pair = remote(p_src, p_recv, p_sem, (i, sibling))
    pair.start()
    o_st[0] = statistics(top_o, total_o, cross_o)
    pair_o = remote(o_st.at[0], o_st.at[1], ost_sem, (i, sibling))
    pair_o.start()
    gather_wait(0)
    gather_start(1)
    total_c, cross_c, acc_c = sums(c, top_c, base_c)
    c_st[0] = statistics(top_c, total_c, cross_c)
    pair_c = remote(c_st.at[0], c_st.at[1], cst_sem, (i, sibling))
    pair_c.start()
    gather_wait(1)
    gather_start(2)
    share_start(0)

    def together(mine, theirs, base):
        best = jnp.maximum(mine[0:1], theirs[0:1])
        scale_mine = jnp.exp2((mine[0:1] - best) * base)
        scale_theirs = jnp.exp2((theirs[0:1] - best) * base)
        return best, mine[1:3] * scale_mine + theirs[1:3] * scale_theirs, scale_mine, scale_theirs

    pair_o.wait_recv()
    best_c, sums_c, scale_mine, scale_theirs = together(c_st[0], o_st[1], base_c)
    own_scale = columns_of(jnp.concatenate([scale_mine, scale_theirs], axis=0))
    pair.wait_recv()
    d_src[...] = (acc_c * own_scale[:, 0:1] + p_recv[...] * own_scale[:, 1:2]).reshape(DEEP, 16, BOT)
    for step in Z_STEPS:
        remote(d_src.at[(z + step) % DEEP], d_recv.at[z], d_sem, z_peer(step)).start()

    pair_c.wait_recv()
    best_o, sums_o, _, _ = together(o_st[0], c_st[1], base_o)
    st_buf[z] = jnp.concatenate(
        [
            jnp.where(core_0, best_c, best_o),
            jnp.where(core_0, best_o, best_c),
            jnp.where(core_0, sums_c[0:1], sums_o[0:1]),
            jnp.where(core_0, sums_o, sums_c),
            jnp.zeros((3, 128), F32),
        ],
        axis=0,
    )
    for step in Z_STEPS:
        remote(st_buf.at[z], st_buf.at[z], c_sem, z_peer(step)).start()
    d_recv[z] = d_src[z]
    count = jnp.full((1, 128), cnt[0, 0], jnp.int32)
    live = lax.broadcasted_iota(jnp.int32, (1, 128), 1) < count
    weight = jnp.where(live, 1.0 / count.astype(F32), 0.0).astype(BF16).astype(F32)

    gather_wait(2)
    gather_start(3)
    share_start(1)
    share_start(2)

    wait_bytes(st_buf.at[pl.ds(0, DEEP - 1)], c_sem.at[1])
    all_top_s, all_top_t = st_buf[:, 0, :], st_buf[:, 1, :]
    max_s = jnp.max(all_top_s, axis=0, keepdims=True)
    max_t = jnp.max(all_top_t, axis=0, keepdims=True)
    scale_s = jnp.exp2((all_top_s - max_s) * STUDENT_2)
    scale_t = jnp.exp2((all_top_t - max_t) * TEACHER_2)
    total_s = jnp.sum(st_buf[:, 2, :] * scale_s, axis=0, keepdims=True)
    total_t = jnp.sum(st_buf[:, 3, :] * scale_t, axis=0, keepdims=True)
    total_x = jnp.sum(st_buf[:, 4, :] * scale_t, axis=0, keepdims=True)
    factor_s = GRAD_SCALE * weight / total_s
    factor_t = GRAD_SCALE * weight / total_t
    tot_buf[0] = jnp.concatenate(
        [max_s * STUDENT_2, factor_s, max_t * TEACHER_2, factor_t, jnp.zeros((4, 128), F32)], axis=0
    )

    for dx, dy in PLANE_STEPS:
        slot = ((SIDE - dx) % SIDE) * SIDE + (SIDE - dy) % SIDE
        remote(tot_buf.at[0], tot_buf.at[slot], t_sem, (plane_peer(dx, dy), p)).start()
    d_col[...] = columns_of(jnp.where(core_0, scale_s * factor_s, scale_t * factor_t))
    wait_bytes(d_recv.at[pl.ds(0, DEEP - 1)], d_sem.at[1])
    scales = d_col[pl.ds(pl.multiple_of(16 * z, 16), 16), :]
    half_grad = d_recv[0] * scales[:, 0:1]
    for k in range(1, DEEP):
        half_grad = half_grad + d_recv[k] * scales[:, k : k + 1]
    h_buf[c] = half_grad
    h_copy = remote(h_buf.at[c], h_buf.at[c], h_sem, (i, sibling))
    h_copy.start()

    hidden_copy.wait_recv()
    hidden = hid[0]
    inverse = lax.rsqrt(jnp.sum(hidden * hidden, axis=1, keepdims=True) + EPSILON)
    h_copy.wait_recv()
    grad = h_buf[0] - h_buf[1]
    inner = jnp.sum(hidden * grad, axis=1, keepdims=True)
    e_buf[z] = (grad * inverse - hidden * inner * (inverse * inverse * inverse)).astype(BF16)
    for step in Z_STEPS:
        remote(e_buf.at[z], e_buf.at[z], e_sem, z_peer(step)).start()

    gather_wait(3)
    share_start(3)
    loss_rows = -(
        STUDENT_SCALE * (total_x / total_t) - STUDENT_SCALE * max_s - jnp.log(total_s)
    )
    loss_ref[...] = weight * loss_rows

    for part in share:
        for copy in part:
            copy.wait_recv()
    wait_bytes(tot_buf.at[pl.ds(1, IMG - 1)], t_sem.at[1])
    g_acc[...] = jnp.zeros_like(g_acc)

    def protos_gradient(dx, carry):
        unit_s = units[0, dx].reshape(SIDE * ROWS, BOT)
        unit_t = units[1, dx].reshape(SIDE * ROWS, BOT)
        raw_s = lax.dot_general(ps_own_t[...], unit_s, CONTRACT_LAST, preferred_element_type=F32)
        raw_t = lax.dot_general(pt_own_t[...], unit_t, CONTRACT_LAST, preferred_element_type=F32)
        totals = tot_buf[pl.ds(SIDE * dx, SIDE)]
        slopes = []
        for q in range(width // 128):
            block = slice(128 * q, 128 * (q + 1))
            center = cen_own_t[block, :]
            line = []
            for dy in range(SIDE):
                lanes = slice(128 * dy, 128 * (dy + 1))
                exp_s = jnp.exp2(raw_s[block, lanes] * STUDENT_2 - totals[dy, 0:1])
                exp_t = jnp.exp2((raw_t[block, lanes] - center) * TEACHER_2 - totals[dy, 2:3])
                line.append((exp_s * totals[dy, 1:2] - exp_t * totals[dy, 3:4]).astype(BF16))
            slopes.append(jnp.concatenate(line, axis=1))
        g_acc[...] += jnp.dot(
            jnp.concatenate(slopes, axis=0), unit_s, preferred_element_type=F32
        )
        return carry

    lax.fori_loop(0, SIDE, protos_gradient, 0)
    g_src[...] = g_acc[...].T.astype(BF16).reshape(IMG, 16, width)
    for dx, dy in PLANE_STEPS:
        target = plane_peer(dx, dy)
        remote(g_src.at[target], gp_h.at[:, own_columns], g_sem, (target, p)).start()
    keep = pltpu.make_async_copy(g_src.at[i], gp_h.at[:, own_columns], load_sem.at[0])
    keep.start()

    wait_bytes(e_buf.at[pl.ds(0, DEEP - 1)], e_sem.at[1])
    grad_hidden = e_buf[...].reshape(ROWS, BOT)
    f_src[...] = (
        lax.dot_general(grad_hidden, rows_s[...], CONTRACT_FIRST, preferred_element_type=F32)
        .astype(BF16)
        .reshape(IMG, 16, BOT)
    )
    for dx, dy in PLANE_STEPS:
        target = plane_peer(dx, dy)
        remote(f_src.at[target], f_recv.at[i], f_sem, (target, p)).start()
    f_recv[i] = f_src[i]

    a1.wait_send()
    wait_bytes(a2_recv, a2_sem.at[0])
    hidden_copy.wait_send()
    wait_bytes(b_buf.at[c, pl.ds(0, DEEP - 1)], b_sem.at[0])
    b2.wait_send()
    pair.wait_send()
    pair_o.wait_send()
    pair_c.wait_send()
    wait_bytes(st_buf.at[pl.ds(0, DEEP - 1)], c_sem.at[0])
    wait_bytes(d_recv.at[pl.ds(0, DEEP - 1)], d_sem.at[0])
    wait_bytes(tot_buf.at[pl.ds(1, IMG - 1)], t_sem.at[0])
    h_copy.wait_send()
    wait_bytes(e_buf.at[pl.ds(0, DEEP - 1)], e_sem.at[0])
    for half in range(2):
        for stage in range(4):
            for copy in gather[half][stage]:
                copy.wait_send()
    for part in share:
        for copy in part:
            copy.wait_send()
    wait_bytes(g_src.at[pl.ds(0, IMG - 1)], g_sem.at[0])
    wait_bytes(f_src.at[pl.ds(0, IMG - 1)], f_sem.at[0])
    keep.wait()

    wait_bytes(f_recv.at[pl.ds(0, IMG - 1)], f_sem.at[1])
    bottleneck = f_recv[0].astype(F32)
    for k in range(1, IMG):
        bottleneck = bottleneck + f_recv[k].astype(F32)
    gb_ref[...] = bottleneck
    wait_bytes(gp_h.at[:, pl.ds(0, (IMG - 1) * width)], g_sem.at[1])


def finish(gp_in, gb_in, loss_in, loss_ref, gp_ref, gb_ref):
    gp_ref[...] = gp_in[...].astype(F32)
    gb_ref[...] = gb_in[...]
    loss_ref[0] = jnp.sum(loss_in[...])


def per_device(
    student_patch_tokens,
    teacher_patch_tokens,
    mask_counts,
    mask_index,
    student_bottleneck,
    teacher_bottleneck,
    student_protos,
    teacher_protos,
    center,
):
    patches, features = student_patch_tokens.shape[1:]
    protos = student_protos.shape[1]
    width = protos // IMG
    in_hbm = pl.BlockSpec(memory_space=pltpu.HBM)
    in_vmem = pl.BlockSpec(memory_space=pltpu.VMEM)
    dma = pltpu.SemaphoreType.DMA
    parts = pl.pallas_call(
        kernel,
        out_shape=(
            jax.ShapeDtypeStruct((BOT // IMG, protos), BF16),
            jax.ShapeDtypeStruct((BOT // IMG, features), F32),
            jax.ShapeDtypeStruct((1, 128), F32),
        ),
        in_specs=[in_hbm] * 9,
        out_specs=(in_hbm, in_vmem, in_vmem),
        scratch_shapes=[
            pltpu.VMEM((patches, features), BF16),
            pltpu.VMEM((patches, features), BF16),
            pltpu.SMEM((1, 1), jnp.int32),
            pltpu.VMEM((1, ROWS), jnp.int32),
            pltpu.VMEM((features, BOT), BF16),
            pltpu.VMEM((features, BOT), BF16),
            pltpu.VMEM((2, BOT, protos), BF16),
            pltpu.VMEM((2, protos // 128, 128), F32),
            pltpu.VMEM((BOT, width), BF16),
            pltpu.VMEM((BOT, width), BF16),
            pltpu.VMEM((ROWS, features), BF16),
            pltpu.VMEM((DEEP, 16, BOT), F32),
            pltpu.VMEM((DEEP, 16, BOT), F32),
            pltpu.VMEM((DEEP, 16, BOT), F32),
            pltpu.VMEM((DEEP - 1, 16, BOT), F32),
            pltpu.VMEM((2, 16, BOT), F32),
            pltpu.VMEM((2, DEEP, 16, BOT), BF16),
            pltpu.VMEM((2, SIDE, SIDE, ROWS, BOT), BF16),
            pltpu.VMEM((2, ROWS, protos), F32),
            pltpu.VMEM((ROWS, BOT), F32),
            pltpu.VMEM((ROWS, BOT), F32),
            pltpu.VMEM((2, 8, 128), F32),
            pltpu.VMEM((2, 8, 128), F32),
            pltpu.VMEM((DEEP, 8, 128), F32),
            pltpu.VMEM((IMG, 8, 128), F32),
            pltpu.VMEM((DEEP, 16, BOT), F32),
            pltpu.VMEM((DEEP, 16, BOT), F32),
            pltpu.VMEM((ROWS, 128), F32),
            pltpu.VMEM((2, 16, BOT), F32),
            pltpu.VMEM((DEEP, 16, BOT), BF16),
            pltpu.VMEM((width, BOT), BF16),
            pltpu.VMEM((width, BOT), BF16),
            pltpu.VMEM((width, 128), F32),
            pltpu.VMEM((width, BOT), F32),
            pltpu.VMEM((IMG, 16, width), BF16),
            pltpu.VMEM((IMG, 16, features), BF16),
            pltpu.VMEM((IMG, 16, features), BF16),
            dma((11,)),
        ]
        + [dma((2,))] * 15
        + [
            dma((16,)),
            dma((16,)),
            dma((8,)),
            dma((8,)),
        ],
        compiler_params=pltpu.CompilerParams(
            collective_id=0, has_side_effects=True, vmem_limit_bytes=56 * 1024 * 1024
        ),
    )(
        student_patch_tokens,
        teacher_patch_tokens,
        mask_counts.reshape(1, 1),
        mask_index,
        student_bottleneck,
        teacher_bottleneck,
        student_protos,
        teacher_protos,
        center.reshape(protos // 128, 128),
    )
    image_loss, grad_protos, grad_bottleneck = pl.pallas_call(
        finish,
        out_shape=(
            jax.ShapeDtypeStruct((1,), F32),
            jax.ShapeDtypeStruct((BOT // IMG, protos), F32),
            jax.ShapeDtypeStruct((BOT // IMG, features), F32),
        ),
        in_specs=[in_vmem] * 3,
        out_specs=(pl.BlockSpec(memory_space=pltpu.SMEM), in_vmem, in_vmem),
    )(*parts)
    return image_loss, grad_protos, grad_bottleneck.T


def solution(mesh):
    placed = (
        P("img", None, "proto"),
        P("img", None, "proto"),
        P("img"),
        P("img", None),
        P("proto", None),
        P("proto", None),
        P(None, "proto"),
        P(None, "proto"),
        P("proto"),
    )
    return jax.shard_map(
        per_device,
        mesh=mesh,
        in_specs=placed,
        out_specs=(P("img"), P("img", "proto"), P("proto", "img")),
        check_vma=False,
    )
```

```python
import math

import jax
import jax.numpy as jnp
from jax import lax
from jax.experimental import pallas as pl
from jax.experimental.pallas import tpu as pltpu
from jax.sharding import PartitionSpec as P

EPSILON = 1e-06
STUDENT_SCALE = 10.0
LOG2E = 1.0 / math.log(2.0)
STUDENT_2 = 10.0 * LOG2E
TEACHER_2 = 25.0 * LOG2E
GRAD_SCALE = 40960.0
MESH = pl.DeviceIdType.MESH
F32 = jnp.float32
BF16 = jnp.bfloat16

SIDE = 4
IMG = 16
DEEP = 8
ROWS = 128
BOT = 256
TILE = 1024
CONTRACT_LAST = (((1,), (1,)), ((), ()))
CONTRACT_FIRST = (((0,), (0,)), ((), ()))

Z_STEPS = (4, 3, 5, 2, 6, 1, 7)
PLANE_STEPS = tuple(
    sorted(
        ((dx, dy) for dx in range(SIDE) for dy in range(SIDE) if dx or dy),
        key=lambda d: -(min(d[0], SIDE - d[0]) + min(d[1], SIDE - d[1])),
    )
)


def wait_bytes(ref, sem):
    pltpu.make_async_copy(ref, ref, sem).wait()


def columns_of(rows):
    pad = jnp.zeros((128 - rows.shape[0], 128), F32)
    return jnp.concatenate([rows, pad], axis=0).T


def kernel(
    tok_s_h,
    tok_t_h,
    cnt_h,
    idx_h,
    bs_h,
    bt_h,
    ps_h,
    pt_h,
    cen_h,
    gp_h,
    gb_h,
    loss_h,
    tok_s,
    tok_t,
    cnt,
    idx,
    bs,
    bt,
    pro,
    cen,
    ps_own,
    pt_own,
    rows_s,
    a1_src,
    a1_recv,
    a2_src,
    a2_recv,
    hid,
    b_buf,
    units,
    raw,
    p_src,
    p_recv,
    o_st,
    c_st,
    st_buf,
    tot_buf,
    d_src,
    d_recv,
    d_col,
    h_buf,
    e_buf,
    ps_own_t,
    pt_own_t,
    cen_own_t,
    g_acc,
    g_src,
    f_src,
    loss,
    load_sem,
    a1_sem,
    a2_sem,
    hid_sem,
    b_sem,
    b2_sem,
    p_sem,
    ost_sem,
    cst_sem,
    c_sem,
    t_sem,
    d_sem,
    h_sem,
    e_sem,
    f_sem,
    g_sem,
    ag_send,
    ag_recv,
    sh_send,
    sh_recv,
):
    i = lax.axis_index("img")
    p = lax.axis_index("proto")
    x, y = i // SIDE, i % SIDE
    z, c = p // 2, p % 2
    width = ps_own.shape[1]
    tiles = pro.shape[2] // TILE
    sibling = p + 1 - 2 * c
    core_0 = c == 0
    o = 1 - c
    base_c = jnp.where(core_0, STUDENT_2, TEACHER_2)
    base_o = jnp.where(core_0, TEACHER_2, STUDENT_2)

    def z_peer(step):
        return (i, ((z + step) % DEEP) * 2 + c)

    def plane_peer(dx, dy):
        return ((x + dx) % SIDE) * SIDE + (y + dy) % SIDE

    def remote(src, dst, sems, device):
        return pltpu.make_async_remote_copy(
            src, dst, sems.at[0], sems.at[1], device_id=device, device_id_type=MESH
        )

    own_columns = pl.ds(pl.multiple_of(i * width, 128), width)
    loads = [
        pltpu.make_async_copy(src, dst, load_sem.at[n])
        for n, (src, dst) in enumerate(
            (
                (idx_h, idx),
                (tok_s_h.at[0], tok_s),
                (bs_h, bs),
                (tok_t_h.at[0], tok_t),
                (bt_h, bt),
                (cen_h, cen.at[1]),
                (ps_h.at[:, own_columns], ps_own),
                (pt_h.at[:, own_columns], pt_own),
                (ps_h, pro.at[0]),
                (pt_h, pro.at[1]),
                (cnt_h, cnt),
            )
        )
    ]
    for load in loads[:5]:
        load.start()

    barrier = pltpu.get_barrier_semaphore()
    pl.semaphore_signal(barrier, inc=1, device_id=(i, sibling), device_id_type=MESH)
    for step in Z_STEPS:
        pl.semaphore_signal(barrier, inc=1, device_id=z_peer(step), device_id_type=MESH)
    for dx, dy in PLANE_STEPS:
        pl.semaphore_signal(barrier, inc=1, device_id=(plane_peer(dx, dy), p), device_id_type=MESH)

    loads[0].wait()
    spread = jnp.broadcast_to(idx[...].astype(F32), (ROWS, ROWS)).T
    patch = lax.broadcasted_iota(jnp.int32, (ROWS, ROWS), 1).astype(F32)
    picker = jnp.concatenate(
        [(spread == patch).astype(F32), (spread == patch + 128.0).astype(F32)], axis=1
    ).astype(BF16)
    loads[1].wait()
    rows_s[...] = jnp.dot(picker, tok_s[...], preferred_element_type=F32).astype(BF16)
    loads[3].wait()
    rows_t = jnp.dot(picker, tok_t[...], preferred_element_type=F32).astype(BF16)
    loads[2].wait()
    part_s = jnp.dot(rows_s[...], bs[...], preferred_element_type=F32)
    loads[4].wait()
    part_t = jnp.dot(rows_t, bt[...], preferred_element_type=F32)
    a1_src[...] = jnp.where(core_0, part_t, part_s).reshape(DEEP, 16, BOT)
    a2_src[...] = jnp.where(core_0, part_s, part_t).reshape(DEEP, 16, BOT)

    pl.semaphore_wait(barrier, 1 + len(Z_STEPS) + len(PLANE_STEPS))

    a1 = remote(a1_src, a1_recv, a1_sem, (i, sibling))
    a1.start()
    a1.wait_recv()
    a2_src[...] = a2_src[...] + a1_recv[...]
    for step in Z_STEPS:
        remote(
            a2_src.at[(z + step) % DEEP], a2_recv.at[step - 1], a2_sem, z_peer(step)
        ).start()

    cen[0] = jnp.zeros_like(cen[0])
    for load in loads[5:]:
        load.start()
    for load in loads[5:8]:
        load.wait()
    ps_own_t[...] = ps_own[...].astype(F32).T.astype(BF16)
    pt_own_t[...] = pt_own[...].astype(F32).T.astype(BF16)
    for q in range(width // 128):
        cen_own_t[pl.ds(128 * q, 128), :] = jnp.broadcast_to(
            cen[1, pl.ds(i * (width // 128) + q, 1), :], (128, 128)
        ).T

    wait_bytes(a2_recv, a2_sem.at[1])
    total = a2_src[z]
    for k in range(DEEP - 1):
        total = total + a2_recv[k]
    inv = lax.rsqrt(jnp.sum(total * total, axis=1, keepdims=True) + EPSILON)
    b_buf[c, z] = (total * inv).astype(BF16)

    for step in Z_STEPS:
        remote(b_buf.at[c, z], b_buf.at[c, z], b_sem, z_peer(step)).start()
    hid[c] = total
    hidden_copy = remote(hid.at[c], hid.at[c], hid_sem, (i, sibling))
    hidden_copy.start()
    for load in loads[8:]:
        load.wait()
    wait_bytes(b_buf.at[c, pl.ds(0, DEEP - 1)], b_sem.at[1])
    b2 = remote(b_buf.at[c], b_buf.at[c], b2_sem, (i, sibling))
    b2.start()
    units[c, 0, 0] = b_buf[c].reshape(ROWS, BOT)

    def gather_copy(half, stage, forward):
        first = stage < 2
        along_x = (half == 0) == first
        step = 1 if forward else SIDE - 1
        base = 64 * half
        if stage % 2 == 0:
            src_slot, dst_slot, rows = 0, (3 if forward else 1), pl.ds(base, 64)
        else:
            src_slot, dst_slot = (3 if forward else 1), 2
            rows = pl.ds(base if forward else base + 32, 32)

        def view(slot):
            if along_x:
                return units.at[c, slot, 0, rows] if first else units.at[c, slot, :, rows]
            return units.at[c, 0, slot, rows] if first else units.at[c, :, slot, rows]

        n = half * 8 + stage * 2 + (0 if forward else 1)
        return pltpu.make_async_remote_copy(
            view(src_slot),
            view(dst_slot),
            ag_send.at[n],
            ag_recv.at[n],
            device_id=(plane_peer(step, 0) if along_x else plane_peer(0, step), p),
            device_id_type=MESH,
        )

    gather = [
        [[gather_copy(half, stage, forward) for forward in (True, False)] for stage in range(4)]
        for half in range(2)
    ]

    def gather_start(stage):
        for half in range(2):
            for copy in gather[half][stage]:
                copy.start()

    def gather_wait(stage):
        for half in range(2):
            for copy in gather[half][stage]:
                copy.wait_recv()

    def share_copy(half, part):
        rows = pl.ds(64 * half, 64)
        if part == 0:
            ref = units.at[c, pl.ds(1, 3), 0, rows] if half == 0 else units.at[c, 0, pl.ds(1, 3), rows]
        else:
            slot = (1, 3, 2)[part - 1]
            ref = units.at[c, :, slot, rows] if half == 0 else units.at[c, slot, :, rows]
        n = half * 4 + part
        return pltpu.make_async_remote_copy(
            ref, ref, sh_send.at[n], sh_recv.at[n], device_id=(i, sibling), device_id_type=MESH
        )

    share = [[share_copy(half, part) for half in range(2)] for part in range(4)]

    def share_start(part):
        for copy in share[part]:
            copy.start()

    gather_start(0)

    def logits(kind):
        def step(j, top):
            columns = pl.ds(pl.multiple_of(j * TILE, TILE), TILE)
            product = jnp.dot(units[kind, 0, 0], pro[kind, :, columns], preferred_element_type=F32)
            for q in range(TILE // 128):
                moved = product[:, 128 * q : 128 * (q + 1)] - cen[
                    kind, pl.ds(j * (TILE // 128) + q, 1), :
                ]
                raw[kind, :, pl.ds(pl.multiple_of(j * TILE + 128 * q, 128), 128)] = moved
                top = jnp.maximum(top, moved)
            return top

        top = lax.fori_loop(0, tiles, step, jnp.full((ROWS, 128), -jnp.inf, F32), unroll=True)
        return jnp.max(top, axis=1, keepdims=True)

    top_c = logits(c)
    b2.wait_recv()
    units[o, 0, 0] = b_buf[o].reshape(ROWS, BOT)
    top_o = logits(o)
    gather_wait(0)
    gather_start(1)

    def sums(kind, top, base):
        shift = top * base

        def step(j, carry):
            total, cross, acc = carry
            parts = []
            for q in range(TILE // 128):
                here = pl.ds(pl.multiple_of(j * TILE + 128 * q, 128), 128)
                power = jnp.exp2(raw[kind, :, here] * base - shift)
                total = total + power
                cross = cross + power * raw[1 - kind, :, here]
                parts.append(power.astype(BF16))
            columns = pl.ds(pl.multiple_of(j * TILE, TILE), TILE)
            acc = acc + lax.dot_general(
                jnp.concatenate(parts, axis=1),
                pro[0, :, columns],
                CONTRACT_LAST,
                preferred_element_type=F32,
            )
            return total, cross, acc

        zero = jnp.zeros((ROWS, 128), F32)
        total, cross, acc = lax.fori_loop(
            0, tiles, step, (zero, zero, jnp.zeros((ROWS, BOT), F32)), unroll=True
        )
        return total, cross, acc

    def statistics(top, total, cross):
        lane = lax.broadcasted_iota(jnp.int32, (ROWS, 128), 1)
        table = jnp.where(lane == 0, top, 0.0)
        for n, value in ((1, total), (2, cross)):
            table = jnp.where(lane == n, jnp.sum(value, axis=1, keepdims=True), table)
        return table.T[:8]

    total_o, cross_o, acc_o = sums(o, top_o, base_o)
    p_src[...] = acc_o
    pair = remote(p_src, p_recv, p_sem, (i, sibling))
    pair.start()
    o_st[0] = statistics(top_o, total_o, cross_o)
    pair_o = remote(o_st.at[0], o_st.at[1], ost_sem, (i, sibling))
    pair_o.start()
    total_c, cross_c, acc_c = sums(c, top_c, base_c)
    c_st[0] = statistics(top_c, total_c, cross_c)
    pair_c = remote(c_st.at[0], c_st.at[1], cst_sem, (i, sibling))
    pair_c.start()

    def together(mine, theirs, base):
        best = jnp.maximum(mine[0:1], theirs[0:1])
        scale_mine = jnp.exp2((mine[0:1] - best) * base)
        scale_theirs = jnp.exp2((theirs[0:1] - best) * base)
        return best, mine[1:3] * scale_mine + theirs[1:3] * scale_theirs, scale_mine, scale_theirs

    pair_o.wait_recv()
    best_c, sums_c, scale_mine, scale_theirs = together(c_st[0], o_st[1], base_c)
    own_scale = columns_of(jnp.concatenate([scale_mine, scale_theirs], axis=0))
    pair.wait_recv()
    d_src[...] = (acc_c * own_scale[:, 0:1] + p_recv[...] * own_scale[:, 1:2]).reshape(DEEP, 16, BOT)
    for step in Z_STEPS:
        remote(d_src.at[(z + step) % DEEP], d_recv.at[z], d_sem, z_peer(step)).start()

    gather_wait(1)
    gather_start(2)
    share_start(0)

    pair_c.wait_recv()
    best_o, sums_o, _, _ = together(o_st[0], c_st[1], base_o)
    st_buf[z] = jnp.concatenate(
        [
            jnp.where(core_0, best_c, best_o),
            jnp.where(core_0, best_o, best_c),
            jnp.where(core_0, sums_c[0:1], sums_o[0:1]),
            jnp.where(core_0, sums_o, sums_c),
            jnp.zeros((3, 128), F32),
        ],
        axis=0,
    )
    for step in Z_STEPS:
        remote(st_buf.at[z], st_buf.at[z], c_sem, z_peer(step)).start()
    d_recv[z] = d_src[z]
    count = jnp.full((1, 128), cnt[0, 0], jnp.int32)
    live = lax.broadcasted_iota(jnp.int32, (1, 128), 1) < count
    weight = jnp.where(live, 1.0 / count.astype(F32), 0.0).astype(BF16).astype(F32)

    gather_wait(2)
    gather_start(3)
    share_start(1)
    share_start(2)

    wait_bytes(st_buf.at[pl.ds(0, DEEP - 1)], c_sem.at[1])
    all_top_s, all_top_t = st_buf[:, 0, :], st_buf[:, 1, :]
    max_s = jnp.max(all_top_s, axis=0, keepdims=True)
    max_t = jnp.max(all_top_t, axis=0, keepdims=True)
    scale_s = jnp.exp2((all_top_s - max_s) * STUDENT_2)
    scale_t = jnp.exp2((all_top_t - max_t) * TEACHER_2)
    total_s = jnp.sum(st_buf[:, 2, :] * scale_s, axis=0, keepdims=True)
    total_t = jnp.sum(st_buf[:, 3, :] * scale_t, axis=0, keepdims=True)
    total_x = jnp.sum(st_buf[:, 4, :] * scale_t, axis=0, keepdims=True)
    factor_s = GRAD_SCALE * weight / total_s
    factor_t = GRAD_SCALE * weight / total_t
    tot_buf[0] = jnp.concatenate(
        [max_s * STUDENT_2, factor_s, max_t * TEACHER_2, factor_t, jnp.zeros((4, 128), F32)], axis=0
    )

    for dx, dy in PLANE_STEPS:
        slot = ((SIDE - dx) % SIDE) * SIDE + (SIDE - dy) % SIDE
        remote(tot_buf.at[0], tot_buf.at[slot], t_sem, (plane_peer(dx, dy), p)).start()
    d_col[...] = columns_of(jnp.where(core_0, scale_s * factor_s, scale_t * factor_t))
    wait_bytes(d_recv.at[pl.ds(0, DEEP - 1)], d_sem.at[1])
    scales = d_col[pl.ds(pl.multiple_of(16 * z, 16), 16), :]
    half_grad = d_recv[0] * scales[:, 0:1]
    for k in range(1, DEEP):
        half_grad = half_grad + d_recv[k] * scales[:, k : k + 1]
    h_buf[c] = half_grad
    h_copy = remote(h_buf.at[c], h_buf.at[c], h_sem, (i, sibling))
    h_copy.start()

    hidden_copy.wait_recv()
    hidden = hid[0]
    inverse = lax.rsqrt(jnp.sum(hidden * hidden, axis=1, keepdims=True) + EPSILON)
    h_copy.wait_recv()
    grad = h_buf[0] - h_buf[1]
    inner = jnp.sum(hidden * grad, axis=1, keepdims=True)
    e_buf[z] = (grad * inverse - hidden * inner * (inverse * inverse * inverse)).astype(BF16)
    for step in Z_STEPS:
        remote(e_buf.at[z], e_buf.at[z], e_sem, z_peer(step)).start()

    gather_wait(3)
    share_start(3)
    loss_rows = -(
        STUDENT_SCALE * (total_x / total_t) - STUDENT_SCALE * max_s - jnp.log(total_s)
    )
    loss[...] = weight * loss_rows
    keep_loss = pltpu.make_async_copy(loss, loss_h, load_sem.at[1])
    keep_loss.start()

    for part in share:
        for copy in part:
            copy.wait_recv()
    wait_bytes(tot_buf.at[pl.ds(1, IMG - 1)], t_sem.at[1])
    g_acc[...] = jnp.zeros_like(g_acc)

    def protos_gradient(dx, carry):
        unit_s = units[0, dx].reshape(SIDE * ROWS, BOT)
        unit_t = units[1, dx].reshape(SIDE * ROWS, BOT)
        raw_s = lax.dot_general(ps_own_t[...], unit_s, CONTRACT_LAST, preferred_element_type=F32)
        raw_t = lax.dot_general(pt_own_t[...], unit_t, CONTRACT_LAST, preferred_element_type=F32)
        totals = tot_buf[pl.ds(SIDE * dx, SIDE)]
        slopes = []
        for q in range(width // 128):
            block = slice(128 * q, 128 * (q + 1))
            center = cen_own_t[block, :]
            line = []
            for dy in range(SIDE):
                lanes = slice(128 * dy, 128 * (dy + 1))
                exp_s = jnp.exp2(raw_s[block, lanes] * STUDENT_2 - totals[dy, 0:1])
                exp_t = jnp.exp2((raw_t[block, lanes] - center) * TEACHER_2 - totals[dy, 2:3])
                line.append((exp_s * totals[dy, 1:2] - exp_t * totals[dy, 3:4]).astype(BF16))
            slopes.append(jnp.concatenate(line, axis=1))
        g_acc[...] += jnp.dot(
            jnp.concatenate(slopes, axis=0), unit_s, preferred_element_type=F32
        )
        return carry

    lax.fori_loop(0, SIDE, protos_gradient, 0, unroll=True)
    g_src[...] = g_acc[...].T.astype(BF16).reshape(IMG, 16, width)
    for dx, dy in PLANE_STEPS:
        target = plane_peer(dx, dy)
        remote(g_src.at[target], gp_h.at[:, own_columns], g_sem, (target, p)).start()
    keep = pltpu.make_async_copy(g_src.at[i], gp_h.at[:, own_columns], load_sem.at[0])
    keep.start()

    wait_bytes(e_buf.at[pl.ds(0, DEEP - 1)], e_sem.at[1])
    grad_hidden = e_buf[...].reshape(ROWS, BOT)
    f_src[...] = (
        lax.dot_general(grad_hidden, rows_s[...], CONTRACT_FIRST, preferred_element_type=F32)
        .astype(BF16)
        .reshape(IMG, 16, BOT)
    )
    for dx, dy in PLANE_STEPS:
        target = plane_peer(dx, dy)
        remote(f_src.at[target], gb_h.at[i], f_sem, (target, p)).start()
    keep_part = pltpu.make_async_copy(f_src.at[i], gb_h.at[i], load_sem.at[2])
    keep_part.start()

    a1.wait_send()
    wait_bytes(a2_recv, a2_sem.at[0])
    hidden_copy.wait_send()
    wait_bytes(b_buf.at[c, pl.ds(0, DEEP - 1)], b_sem.at[0])
    b2.wait_send()
    pair.wait_send()
    pair_o.wait_send()
    pair_c.wait_send()
    wait_bytes(st_buf.at[pl.ds(0, DEEP - 1)], c_sem.at[0])
    wait_bytes(d_recv.at[pl.ds(0, DEEP - 1)], d_sem.at[0])
    wait_bytes(tot_buf.at[pl.ds(1, IMG - 1)], t_sem.at[0])
    h_copy.wait_send()
    wait_bytes(e_buf.at[pl.ds(0, DEEP - 1)], e_sem.at[0])
    for half in range(2):
        for stage in range(4):
            for copy in gather[half][stage]:
                copy.wait_send()
    for part in share:
        for copy in part:
            copy.wait_send()
    wait_bytes(g_src.at[pl.ds(0, IMG - 1)], g_sem.at[0])
    wait_bytes(f_src.at[pl.ds(0, IMG - 1)], f_sem.at[0])
    keep.wait()

    keep_loss.wait()
    keep_part.wait()
    wait_bytes(gp_h.at[:, pl.ds(0, (IMG - 1) * width)], g_sem.at[1])
    wait_bytes(gb_h.at[pl.ds(0, IMG - 1)], f_sem.at[1])


def finish(gp_in, gb_in, loss_in, loss_ref, gp_ref, gb_ref):
    gp_ref[...] = gp_in[...].astype(F32)
    total = gb_in[0].astype(F32)
    for k in range(1, IMG):
        total = total + gb_in[k].astype(F32)
    gb_ref[...] = total
    loss_ref[0] = jnp.sum(loss_in[...])


def per_device(
    student_patch_tokens,
    teacher_patch_tokens,
    mask_counts,
    mask_index,
    student_bottleneck,
    teacher_bottleneck,
    student_protos,
    teacher_protos,
    center,
):
    patches, features = student_patch_tokens.shape[1:]
    protos = student_protos.shape[1]
    width = protos // IMG
    in_hbm = pl.BlockSpec(memory_space=pltpu.HBM)
    in_vmem = pl.BlockSpec(memory_space=pltpu.VMEM)
    dma = pltpu.SemaphoreType.DMA
    parts = pl.pallas_call(
        kernel,
        out_shape=(
            jax.ShapeDtypeStruct((BOT // IMG, protos), BF16),
            jax.ShapeDtypeStruct((IMG, BOT // IMG, features), BF16),
            jax.ShapeDtypeStruct((1, 128), F32),
        ),
        in_specs=[in_hbm] * 9,
        out_specs=(in_hbm, in_hbm, in_hbm),
        scratch_shapes=[
            pltpu.VMEM((patches, features), BF16),
            pltpu.VMEM((patches, features), BF16),
            pltpu.SMEM((1, 1), jnp.int32),
            pltpu.VMEM((1, ROWS), jnp.int32),
            pltpu.VMEM((features, BOT), BF16),
            pltpu.VMEM((features, BOT), BF16),
            pltpu.VMEM((2, BOT, protos), BF16),
            pltpu.VMEM((2, protos // 128, 128), F32),
            pltpu.VMEM((BOT, width), BF16),
            pltpu.VMEM((BOT, width), BF16),
            pltpu.VMEM((ROWS, features), BF16),
            pltpu.VMEM((DEEP, 16, BOT), F32),
            pltpu.VMEM((DEEP, 16, BOT), F32),
            pltpu.VMEM((DEEP, 16, BOT), F32),
            pltpu.VMEM((DEEP - 1, 16, BOT), F32),
            pltpu.VMEM((2, 16, BOT), F32),
            pltpu.VMEM((2, DEEP, 16, BOT), BF16),
            pltpu.VMEM((2, SIDE, SIDE, ROWS, BOT), BF16),
            pltpu.VMEM((2, ROWS, protos), F32),
            pltpu.VMEM((ROWS, BOT), F32),
            pltpu.VMEM((ROWS, BOT), F32),
            pltpu.VMEM((2, 8, 128), F32),
            pltpu.VMEM((2, 8, 128), F32),
            pltpu.VMEM((DEEP, 8, 128), F32),
            pltpu.VMEM((IMG, 8, 128), F32),
            pltpu.VMEM((DEEP, 16, BOT), F32),
            pltpu.VMEM((DEEP, 16, BOT), F32),
            pltpu.VMEM((ROWS, 128), F32),
            pltpu.VMEM((2, 16, BOT), F32),
            pltpu.VMEM((DEEP, 16, BOT), BF16),
            pltpu.VMEM((width, BOT), BF16),
            pltpu.VMEM((width, BOT), BF16),
            pltpu.VMEM((width, 128), F32),
            pltpu.VMEM((width, BOT), F32),
            pltpu.VMEM((IMG, 16, width), BF16),
            pltpu.VMEM((IMG, 16, features), BF16),
            pltpu.VMEM((1, 128), F32),
            dma((11,)),
        ]
        + [dma((2,))] * 15
        + [
            dma((16,)),
            dma((16,)),
            dma((8,)),
            dma((8,)),
        ],
        compiler_params=pltpu.CompilerParams(
            collective_id=0, has_side_effects=True, vmem_limit_bytes=56 * 1024 * 1024
        ),
    )(
        student_patch_tokens,
        teacher_patch_tokens,
        mask_counts.reshape(1, 1),
        mask_index,
        student_bottleneck,
        teacher_bottleneck,
        student_protos,
        teacher_protos,
        center.reshape(protos // 128, 128),
    )
    image_loss, grad_protos, grad_bottleneck = pl.pallas_call(
        finish,
        out_shape=(
            jax.ShapeDtypeStruct((1,), F32),
            jax.ShapeDtypeStruct((BOT // IMG, protos), F32),
            jax.ShapeDtypeStruct((BOT // IMG, features), F32),
        ),
        in_specs=[in_vmem] * 3,
        out_specs=(pl.BlockSpec(memory_space=pltpu.SMEM), in_vmem, in_vmem),
    )(*parts)
    return image_loss, grad_protos, grad_bottleneck.T


def solution(mesh):
    placed = (
        P("img", None, "proto"),
        P("img", None, "proto"),
        P("img"),
        P("img", None),
        P("proto", None),
        P("proto", None),
        P(None, "proto"),
        P(None, "proto"),
        P("proto"),
    )
    return jax.shard_map(
        per_device,
        mesh=mesh,
        in_specs=placed,
        out_specs=(P("img"), P("img", "proto"), P("proto", "img")),
        check_vma=False,
    )
```
